128 devices in a mesh: row: 8 (over y, core), col: 16 (over x, z).
Axes of the slice: x: 4, y: 4, z: 4, core: 2. Of those that a mesh axis runs over, the one named last changes fastest.
Arguments:
- grad_out: bfloat16 [8, 16, 16, 16, 1024], P('row', 'col'), may hold values from -6 to 6
- block_in: bfloat16 [8, 16, 16, 16, 1024], P('row', 'col'), may hold values from -6 to 6
- mid: bfloat16 [8, 16, 16, 16, 1024], P('row', 'col'), may hold values from -6 to 6
- qkv: bfloat16 [8, 16, 16, 16, 3, 1024], P('row', 'col'), may hold values from -8 to 8
- gates: float32 [8, 16, 16, 16, 2], P('row', 'col'), may hold values from 0.05 to 1
- expert_ids: int32 [8, 16, 16, 16, 2], P('row', 'col'), may hold values from 0 to 31, all different within a row; in each aligned block of 256 rows (0 to 255, 256 to 511, ..., all dimensions but the last counted through in order) at most 32 rows name the same one
- w_in: bfloat16 [128, 1024, 1024], P(('row', 'col')), may hold values from -0.1875 to 0.1875
- w_out: bfloat16 [128, 1024, 1024], P(('row', 'col')), may hold values from -0.09375 to 0.09375
- w_qkv: bfloat16 [1024, 3072], replicated, may hold values from -0.1875 to 0.1875
- w_proj: bfloat16 [1024, 1024], replicated, may hold values from -0.1875 to 0.1875
- norm1: float32 [1024], replicated, may hold values from 0.5 to 1.5
- norm2: float32 [1024], replicated, may hold values from 0.5 to 1.5
Outputs:
- grad_in: bfloat16 [8, 16, 16, 16, 1024], P('row', 'col')
The draws below stay inside these ranges and needn't reach their ends.
Inputs may be any that keep to these rules, and one draw needn't show every extreme that they name: `expert_ids`: among the 256 tokens of one device no expert is named more than 32 times, and in every draw some device names some expert exactly 32 times; the two experts of a token differ.
All inputs are finite; a program needn't handle non-finite values.
Results may differ from the reference program's by a relative error of at most 0.02.
Values may be sent and summed in bfloat16 or wider, within the bound.
A program may use at most 128 MiB of HBM per device.

```python
import math
import jax
import jax.numpy as jnp
import numpy as np
from jax import lax

D = 1024
HEADS = 32
E = 32
FF = 4096
WIN = 16
C = 32
OWNERS = 128
FFP = 1024
N_ROW = 8
N_COL = 16


def draw_qkv(key, part):
    key = jax.random.fold_in(key, 11)
    shape = (N_ROW, N_COL, WIN, WIN, 3, D)
    base = jnp.clip(jax.random.normal(key, shape, jnp.float32), -8.0, 8.0)
    return base.astype(jnp.bfloat16)


def block_levels(key, extent, split, low, high):
    factor_of = 1.0
    for axis_at, blocks in split:
        steps = jax.random.uniform(jax.random.fold_in(jax.random.fold_in(key, 6), axis_at), (blocks,), jnp.float32, low / len(split), high / len(split))
        factor_of = factor_of * jnp.repeat(jnp.exp(steps), extent[axis_at] // blocks).reshape((-1,) + (1,) * (len(extent) - 1 - axis_at))
    return factor_of


def assign_block(key, own, number, rows, count, top, reach, slope):
    order = jax.random.permutation(key, count)
    crowded, common = portions_of(count, rows * top, reach, slope, True), portions_of(count, rows * top, reach, slope, False)
    places = jnp.arange(count)

    def named(tallies, turn):
        used = int((tallies > 0).sum())
        fixed = max(1, used // 4)
        shifted = fixed + (places - fixed + turn * (used - fixed)) % max(1, count - fixed)
        return jnp.zeros((count,), jnp.int32).at[order[jnp.where(places < fixed, places, shifted)]].set(jnp.asarray(tallies, jnp.int32))

    tallies = jnp.where(number % 4 == 0, named(crowded, number // 4), named(common, number - number // 4 - 1))
    mixed = jax.random.permutation(jax.random.fold_in(own, 3), count)
    giver, receiver = mixed[0:count // 2 * 2:2], mixed[1:count // 2 * 2:2]
    margin = jnp.minimum(tallies[giver] - 1, reach - tallies[receiver]) // 2
    margin = jnp.where((giver == order[0]) | (receiver == order[0]) | (tallies[receiver] == 0), 0, jnp.maximum(margin, 0))
    shifted = jax.random.randint(jax.random.fold_in(own, 4), (count // 2,), 0, 1 << 20) % (margin + 1)
    tallies = tallies.at[giver].add(-shifted).at[receiver].add(shifted)
    members = jnp.searchsorted(jnp.cumsum(tallies), jnp.arange(rows * top), side="right").astype(jnp.int32)
    table = members.reshape(top, rows).T
    table = table[jax.random.permutation(jax.random.fold_in(own, 1), rows)]
    turn = jax.random.randint(jax.random.fold_in(own, 2), (rows, 1), 0, top)
    return jnp.take_along_axis(table, (jnp.arange(top)[None, :] + turn) % top, axis=1)


def portions_of(number_of, total, most, lean, full):
    portions = [(1 << 20) // math.isqrt(grade ** lean) + 1 for grade in range(1, number_of + 1)]
    largest = most if full else min(most, max(-(-total // number_of), total * portions[0] // sum(portions)))
    least = 1 if total - largest >= number_of - 1 else 0
    given, surplus = [largest] + [least] * (number_of - 1), total - largest - least * (number_of - 1)
    while surplus > 0:
        candidates = [i for i in range(1, number_of) if given[i] < largest] or [i for i in range(1, number_of) if given[i] < most]
        mass, left = sum([portions[i] for i in candidates]), surplus
        for i in candidates:
            extra = min(most - given[i], max(1, left * portions[i] // mass), surplus)
            given[i] = given[i] + extra
            surplus = surplus - extra
    return np.array(given)


def noise(own_key, shape, scale, most, pieces=(), kind=jnp.bfloat16):
    values = scale * jax.random.normal(own_key, shape, jnp.float32)
    if pieces:
        values = values * block_levels(own_key, shape, pieces, -0.22, 0.18)
    return jnp.clip(values, -most, most).astype(kind)


def setup_inputs(seed: int = 0) -> dict:
    key_list = jax.random.split(jax.random.key(seed), 13)
    grad_out = noise(key_list[0], (N_ROW, N_COL, WIN, WIN, D), 1.0, 6.0, ((0, 8), (1, 16)))
    block_in = noise(key_list[1], (N_ROW, N_COL, WIN, WIN, D), 1.0, 6.0, ((0, 8), (1, 16)))
    mid = noise(key_list[2], (N_ROW, N_COL, WIN, WIN, D), 1.0, 6.0, ((0, 8), (1, 16)))
    qkv = draw_qkv(jax.random.fold_in(key_list[12], 71), 0)
    gates = jnp.clip(0.05 + 0.95 * jax.random.uniform(key_list[4], (N_ROW, N_COL, WIN, WIN, 2), jnp.float32) ** block_levels(key_list[4], (N_ROW, N_COL, WIN, WIN, 2), ((0, 8), (1, 16)), -0.2, 0.2), 0.05, 1.0)
    expert_ids_keys = jax.random.split(jax.random.fold_in(key_list[5], 1), N_ROW * N_COL * WIN * WIN // (WIN * WIN))
    expert_ids_turns = jax.random.permutation(jax.random.fold_in(key_list[5], 3), N_ROW * N_COL * WIN * WIN // (WIN * WIN))
    expert_ids = jax.vmap(lambda own, number: assign_block(jax.random.fold_in(key_list[5], 2), own, number, WIN * WIN, E, 2, C, 2))(expert_ids_keys, expert_ids_turns).reshape((N_ROW, N_COL, WIN, WIN, 2))
    w_in = noise(key_list[6], (OWNERS, D, FFP), D ** -0.5, 0.1875, ((0, 128),))
    w_out = noise(key_list[7], (OWNERS, FFP, D), FF ** -0.5, 0.09375, ((0, 128),))
    w_qkv = noise(key_list[8], (D, 3 * D), D ** -0.5, 0.1875)
    w_proj = noise(key_list[9], (D, D), D ** -0.5, 0.1875)
    norm1 = jnp.clip(1.0 + 0.1 * jax.random.normal(key_list[10], (D,), jnp.float32), 0.5, 1.5)
    norm2 = jnp.clip(1.0 + 0.1 * jax.random.normal(key_list[11], (D,), jnp.float32), 0.5, 1.5)
    return dict(grad_out=grad_out, block_in=block_in, mid=mid, qkv=qkv, gates=gates, expert_ids=expert_ids, w_in=w_in, w_out=w_out, w_qkv=w_qkv, w_proj=w_proj, norm1=norm1, norm2=norm2)


EPSILON = 1e-05

def layer_stats(values):
    floats = values.astype(jnp.float32)
    centred = floats - lax.optimization_barrier(jnp.mean(floats, -1, keepdims=True))
    inverse = lax.rsqrt(lax.optimization_barrier(jnp.mean(centred * centred, -1, keepdims=True)) + EPSILON)
    return (centred * inverse, inverse)

def norm_back(upstream, normal_hat, inverse, gain):
    scaled_up = upstream * gain.astype(jnp.float32)
    first = lax.optimization_barrier(jnp.mean(scaled_up, -1, keepdims=True))
    second = lax.optimization_barrier(jnp.mean(scaled_up * normal_hat, -1, keepdims=True))
    return inverse * (scaled_up - first - normal_hat * second)

def gelu_slope(values):
    return 0.5 * (1.0 + lax.erf(values * 0.7071067811865476)) + values * jnp.exp(-0.5 * values * values) * 0.3989422804014327

def window_back(items):
    window_data, labels = items
    tokens_in = window_data.shape[0]
    head_size = D // HEADS
    scale = head_size ** (-0.5)
    parts = window_data.astype(jnp.float32).reshape(tokens_in, 4, HEADS, head_size)
    query = parts[:, 0]
    key_rows = parts[:, 1]
    value_rows = parts[:, 2]
    out_grad = parts[:, 3]
    scores = jnp.einsum('qhd,khd->hqk', query, key_rows) * scale
    allowed = (labels[:, None] == labels[None, :])[None, :, :]
    highest = lax.optimization_barrier(jnp.max(jnp.where(allowed, scores, -1e+30), -1, keepdims=True))
    expo = jnp.exp(jnp.where(allowed, scores - highest, -1e+30))
    probs = expo / lax.optimization_barrier(jnp.sum(expo, -1, keepdims=True))
    probs_b = probs.astype(jnp.bfloat16).astype(jnp.float32)
    value_grad = jnp.einsum('hqk,qhd->khd', probs_b, out_grad).astype(jnp.bfloat16)
    prob_grad = jnp.einsum('qhd,khd->hqk', out_grad, value_rows)
    row_total = lax.optimization_barrier(jnp.sum(probs * prob_grad, -1, keepdims=True))
    score_grad = (probs * (prob_grad - row_total)).astype(jnp.bfloat16).astype(jnp.float32)
    query_grad = (jnp.einsum('hqk,khd->qhd', score_grad, key_rows) * scale).astype(jnp.bfloat16)
    key_grad = (jnp.einsum('hqk,qhd->khd', score_grad, query) * scale).astype(jnp.bfloat16)
    return jnp.stack((query_grad, key_grad, value_grad), 1).reshape(tokens_in, 3, D)

def to_grid(array):
    moved = jnp.swapaxes(array, 1, 2)
    return moved.reshape((N_ROW * WIN, N_COL * WIN) + array.shape[4:])

def to_windows(array):
    split_up = array.reshape((N_ROW, WIN, N_COL, WIN) + array.shape[2:])
    return jnp.swapaxes(split_up, 1, 2)

def reference(grad_out, block_in, mid, qkv, gates, expert_ids, w_in, w_out, w_qkv, w_proj, norm1, norm2):
    count = WIN * WIN
    devices = N_ROW * N_COL
    group = devices // E
    width = FF // group
    half = WIN // 2
    grad_rows = grad_out.reshape(devices * count, D)
    mid_hat, mid_inverse = layer_stats(mid.reshape(devices * count, D))
    normed = (mid_hat * norm2).astype(jnp.bfloat16)
    sent_grad = (gates.reshape(devices * count, 2)[:, :, None] * grad_rows.astype(jnp.float32)[:, None, :]).astype(jnp.bfloat16).reshape(devices * count * 2, D)
    choices_all = expert_ids.reshape(devices, count * 2).astype(jnp.int32)
    expert_hot = (choices_all[:, :, None] == jnp.arange(E, dtype=jnp.int32)[None, None, :]).astype(jnp.int32)
    slot_rank = lax.optimization_barrier(jnp.sum((jnp.cumsum(expert_hot, 1) - 1) * expert_hot, -1)).astype(jnp.int32)
    pair_index = jnp.arange(devices * count * 2, dtype=jnp.int32).reshape(devices, count * 2)
    source = jnp.broadcast_to(jnp.arange(devices, dtype=jnp.int32)[:, None], (devices, count * 2))
    table = jnp.full((E, devices, C), -1, jnp.int32).at[choices_all, source, slot_rank].set(pair_index)
    w_in_four = w_in.reshape(E, group, D, width)
    w_out_four = w_out.reshape(E, group, width, D)

    def expert_step(total, items):
        rows, first_w, second_w = items
        valid = rows >= 0
        safe = jnp.where(valid, rows, 0).astype(jnp.int32)
        normed_rows = normed[safe // 2]
        grad_part = sent_grad[safe]
        first_full = jnp.swapaxes(first_w, 0, 1).reshape(D, group * width)
        second_full = second_w.reshape(group * width, D)
        pre = jnp.dot(normed_rows, first_full, preferred_element_type=jnp.float32)
        act_grad = jnp.dot(grad_part, second_full.T, preferred_element_type=jnp.float32)
        pre_grad = (act_grad * gelu_slope(pre)).astype(jnp.bfloat16)
        shares = jnp.einsum('rgf,gdf->grd', pre_grad.reshape(-1, group, width).astype(jnp.float32), first_w.astype(jnp.float32)).astype(jnp.bfloat16)
        summed = lax.optimization_barrier(jnp.sum(shares.astype(jnp.float32), 0))
        summed = jnp.where(valid[:, None], summed, jnp.zeros((), jnp.float32))
        return (total.at[safe // 2].add(summed), None)
    normed_grad, _ = lax.scan(expert_step, jnp.zeros((devices * count, D), jnp.float32), (table.reshape(E, devices * C), w_in_four, w_out_four))
    mid_grad = (grad_rows.astype(jnp.float32) + norm_back(normed_grad, mid_hat, mid_inverse, norm2)).astype(jnp.bfloat16)
    context_grad = jnp.dot(mid_grad, w_proj.T, preferred_element_type=jnp.float32).astype(jnp.bfloat16)
    stacked = jnp.concatenate((qkv, context_grad.reshape(N_ROW, N_COL, WIN, WIN, 1, D)), 4)
    rolled = jnp.roll(to_grid(stacked), (-half, -half), (0, 1))
    windows = to_windows(rolled).reshape(devices, count, 4, D)
    inner = jnp.arange(WIN) >= half
    row_flag = ((jnp.arange(N_ROW)[:, None] == N_ROW - 1) & inner[None, :]).astype(jnp.int32)
    col_flag = ((jnp.arange(N_COL)[:, None] == N_COL - 1) & inner[None, :]).astype(jnp.int32)
    labels = row_flag[:, None, :, None] * 2 + col_flag[None, :, None, :]
    labels = labels.reshape(devices, count)
    window_grads = lax.map(window_back, (windows, labels))
    unrolled = jnp.roll(to_grid(window_grads.reshape(N_ROW, N_COL, WIN, WIN, 3, D)), (half, half), (0, 1))
    qkv_grad = to_windows(unrolled).reshape(devices * count, 3 * D)
    input_normed_grad = jnp.dot(qkv_grad, w_qkv.T, preferred_element_type=jnp.float32)
    in_hat, in_inverse = layer_stats(block_in.reshape(devices * count, D))
    result = mid_grad.astype(jnp.float32) + norm_back(input_normed_grad, in_hat, in_inverse, norm1)
    return result.astype(jnp.bfloat16).reshape(N_ROW, N_COL, WIN, WIN, D)
```

```python
import jax
import jax.numpy as jnp
from jax import lax
from jax.experimental import pallas as pl
from jax.experimental.pallas import tpu as pltpu
from jax.sharding import PartitionSpec as P

HEADS = 32
E = 32
C = 32
EPSILON = 1e-05
MESH = pl.DeviceIdType.MESH
F32 = jnp.float32
BF16 = jnp.bfloat16
HID = 512
PIECES = 8


def from_behind(block, axis, distance):
    devices = range(lax.axis_size(axis))
    route = [((i - distance) % len(devices), i) for i in devices]
    return lax.ppermute(block, axis, route)


def layer_stats(values):
    floats = values.astype(F32)
    centred = floats - jnp.mean(floats, -1, keepdims=True)
    inverse = lax.rsqrt(jnp.mean(centred * centred, -1, keepdims=True) + EPSILON)
    return (centred * inverse, inverse)


def norm_back(upstream, normal_hat, inverse, gain):
    scaled_up = upstream * gain
    first = jnp.mean(scaled_up, -1, keepdims=True)
    second = jnp.mean(scaled_up * normal_hat, -1, keepdims=True)
    return inverse * (scaled_up - first - normal_hat * second)


def gelu_slope(values):
    return (
        0.5 * (1.0 + lax.erf(values * 0.7071067811865476))
        + values * jnp.exp(-0.5 * values * values) * 0.3989422804014327
    )


def dot(a, b, contract=(1, 0)):
    return lax.dot_general(
        a, b, (((contract[0],), (contract[1],)), ((), ())), preferred_element_type=F32
    )


def to_quadrants(x):
    n = x.shape[-1]
    parts = x.reshape(2, 8, 2, 8, n)
    return jnp.concatenate(
        [parts[a, :, b].reshape(64, n) for a in range(2) for b in range(2)], 0
    )


def from_quadrants(x):
    n = x.shape[-1]
    parts = x.reshape(2, 2, 8, 8, n)
    rows = []
    for a in range(2):
        for i in range(8):
            rows.append(jnp.concatenate([parts[a, 0, i], parts[a, 1, i]], 0))
    return jnp.concatenate(rows, 0)


def position():
    row, col = lax.axis_index("row"), lax.axis_index("col")
    return lax.div(col, 4), lax.div(row, 2), lax.rem(row, 2), lax.rem(col, 4)


def place(x, y, c, z):
    return (2 * y + c, 4 * x + z)


def moe_kernel(
    mid_ref,
    grad_ref,
    gates_ref,
    ids_ref,
    w_in_ref,
    w_out_ref,
    norm2_ref,
    out_ref,
    w_first,
    w_second,
    outgoing,
    arrived,
    total,
    ret_out,
    ret_in,
    choice,
    w_send,
    w_recv,
    d_send,
    d_recv,
    r_send,
    r_recv,
):
    x, y, c, z = position()
    pair = lax.div(z, 2)
    u = z + 1 - 2 * lax.rem(z, 2)
    w = 3 - z
    v = 3 - u
    other = 1 - c
    twin = place(x, y, other, z)
    me = 8 * y + 4 * pair + x

    def member(e):
        ex, ey, eb = lax.rem(e, 4), lax.div(e, 8), lax.rem(lax.div(e, 4), 2)
        differs = lax.rem(eb + pair, 2)
        return place(ex, ey, c, z + differs * (3 - 2 * z))

    barrier = pltpu.get_barrier_semaphore()

    def greet(e, carry):
        @pl.when(e != me)
        def _():
            pl.semaphore_signal(barrier, inc=1, device_id=member(e), device_id_type=MESH)

        return carry

    lax.fori_loop(0, E, greet, 0)
    for where in (twin, place(x, y, 0, u), place(x, y, 1, u), place(x, y, other, w)):
        pl.semaphore_signal(barrier, inc=1, device_id=where, device_id_type=MESH)
    pl.semaphore_wait(barrier, E - 1 + 4)

    def source(which, h):
        if which == 0:
            return w_in_ref.at[:, pl.ds(h * HID, HID)]
        return w_out_ref.at[pl.ds(h * HID, HID), :]

    store = (w_first, w_second)

    def ship(which, src, piece, send_at, where):
        return pltpu.make_async_remote_copy(
            src_ref=src,
            dst_ref=store[which].at[piece],
            send_sem=w_send.at[which, send_at],
            recv_sem=w_recv.at[which, piece],
            device_id=where,
            device_id_type=MESH,
        )

    def local(which, h):
        piece = 2 * z + h
        return pltpu.make_async_copy(
            source(which, h), store[which].at[piece], w_recv.at[which, piece]
        )

    inside = c == pair

    @pl.when(inside)
    def _():
        for h in range(2):
            for which in range(2):
                ship(which, source(which, h), 2 * z + h, h, place(x, y, h, u)).start()
        for h in range(2):
            for which in range(2):
                ship(which, source(which, h), 2 * z + h, 2 + h, twin).start()
                local(which, h).start()

    @pl.when(jnp.logical_not(inside))
    def _():
        for h in range(2):
            for which in range(2):
                ship(which, source(which, h), 2 * z + h, h, place(x, y, h, w)).start()

    norm2 = norm2_ref[...]
    grad = to_quadrants(grad_ref[...].astype(F32))
    mid_hat, mid_inverse = layer_stats(to_quadrants(mid_ref[...].astype(F32)))
    normed = (mid_hat * norm2).astype(BF16)
    gates = gates_ref[...]
    ids = ids_ref[...]
    sent = [(gates[:, k : k + 1] * grad).astype(BF16) for k in range(2)]
    lanes = lax.broadcasted_iota(jnp.int32, (256, E), 1)
    hots = [ids[:, k : k + 1] == lanes for k in range(2)]
    before = (
        lax.broadcasted_iota(jnp.int32, (256, 256), 0)
        > lax.broadcasted_iota(jnp.int32, (256, 256), 1)
    ).astype(BF16)
    hot_f = [h.astype(F32) for h in hots]
    ranks = [dot(before, h.astype(BF16)) for h in hot_f]
    ranks[1] = ranks[1] + jnp.sum(hot_f[0], 0, keepdims=True)
    slots = [
        ids[:, k : k + 1] * C
        + jnp.sum(hot_f[k] * ranks[k], 1, keepdims=True).astype(jnp.int32)
        for k in range(2)
    ]
    wide = lax.broadcasted_iota(jnp.int32, (256, E * C), 1)
    choice[...] = ((slots[0] == wide) | (slots[1] == wide)).astype(BF16)

    def ship_rows(e):
        return pltpu.make_async_remote_copy(
            src_ref=outgoing.at[e],
            dst_ref=arrived.at[me],
            send_sem=d_send.at[e],
            recv_sem=d_recv.at[me],
            device_id=member(e),
            device_id_type=MESH,
        )

    def keep_rows():
        return pltpu.make_async_copy(outgoing.at[me], arrived.at[me], d_recv.at[me])

    narrow = lax.broadcasted_iota(jnp.int32, (256, 256), 1)

    def dispatch(step, carry):
        block = lax.rem(y + step, 4)
        base = block * 256
        picks = [(slots[k] == narrow + base).astype(BF16) for k in range(2)]
        rows_n = dot(picks[0] + picks[1], normed, (0, 0))
        rows_g = dot(picks[0], sent[0], (0, 0)) + dot(picks[1], sent[1], (0, 0))
        outgoing[pl.ds(block * 8, 8), 0] = rows_n.astype(BF16).reshape(8, C, 1024)
        outgoing[pl.ds(block * 8, 8), 1] = rows_g.astype(BF16).reshape(8, C, 1024)

        def send_one(k, carry):
            e = block * 8 + lax.rem(4 * pair + x + k, 8)

            @pl.when(e != me)
            def _():
                ship_rows(e).start()

            @pl.when(e == me)
            def _():
                keep_rows().start()

            return carry

        return lax.fori_loop(0, 8, send_one, carry)

    lax.fori_loop(0, 4, dispatch, 0)
    total[...] = jnp.zeros_like(total)

    def landed(which, piece):
        pltpu.make_async_copy(
            store[which].at[piece], store[which].at[piece], w_recv.at[which, piece]
        ).wait()

    def pass_on(piece, send_at, targets):
        for which in range(2):
            landed(which, piece)
            for n, where in enumerate(targets):
                ship(which, store[which].at[piece], piece, send_at + n, where).start()

    def product(piece, rows, begin):
        count = rows // C
        at = pl.ds(begin, count)
        normed_rows = arrived[at, 0].reshape(rows, 1024)
        grad_rows = arrived[at, 1].reshape(rows, 1024)
        first, second = w_first[piece], w_second[piece]
        pre = dot(normed_rows, first)
        act_grad = dot(grad_rows, second, (1, 1))
        pre_grad = (act_grad * gelu_slope(pre)).astype(BF16)
        return dot(pre_grad, first, (1, 1))

    def whole(piece, rows=512):
        def one(step, carry):
            at = pl.ds(pl.multiple_of(step * rows, rows), rows)
            total[at] = total[at] + product(piece, rows, step * (rows // C))
            return carry

        lax.fori_loop(0, 1024 // rows, one, 0)

    pass_on(2 * w + c, 4, (place(x, y, c, u), twin))
    pass_on(2 * u + c, 6, (twin,))

    def rows_landed(m, carry):
        pltpu.make_async_copy(arrived.at[m], arrived.at[m], d_recv.at[m]).wait()
        return carry

    lax.fori_loop(0, E, rows_landed, 0)
    for h in range(2):
        for which in range(2):
            landed(which, 2 * z + h)
        whole(2 * z + h)
    whole(2 * u + c)
    whole(2 * w + c)
    for which in range(2):
        landed(which, 2 * u + other)
    whole(2 * u + other)
    for which in range(2):
        landed(which, 2 * w + other)
    whole(2 * w + other)
    pass_on(2 * v + c, 7, (twin,))
    whole(2 * v + c)
    for which in range(2):
        landed(which, 2 * v + other)

    def ship_back(m):
        return pltpu.make_async_remote_copy(
            src_ref=ret_out.at[m],
            dst_ref=ret_in.at[me],
            send_sem=r_send.at[m],
            recv_sem=r_recv.at[me],
            device_id=member(m),
            device_id_type=MESH,
        )

    def last(step, carry):
        block = lax.rem(y + step, 4)
        at = pl.ds(pl.multiple_of(block * 256, 256), 256)
        done = total[at] + product(2 * v + other, 256, block * 8)
        ret_out[pl.ds(block * 8, 8)] = done.astype(BF16).reshape(8, C, 1024)

        def send_one(k, carry):
            m = block * 8 + lax.rem(4 * pair + x + k, 8)

            @pl.when(m != me)
            def _():
                ship_back(m).start()

            @pl.when(m == me)
            def _():
                pltpu.make_async_copy(
                    ret_out.at[me], ret_in.at[me], r_recv.at[me]
                ).start()

            return carry

        return lax.fori_loop(0, 8, send_one, carry)

    lax.fori_loop(0, 4, last, 0)

    def back_landed(m, carry):
        pltpu.make_async_copy(ret_in.at[m], ret_in.at[m], r_recv.at[m]).wait()
        return carry

    lax.fori_loop(0, E, back_landed, 0)
    normed_grad = dot(choice[...], ret_in[...].reshape(E * C, 1024))
    mid_grad = grad + norm_back(normed_grad, mid_hat, mid_inverse, norm2)
    out_ref[...] = from_quadrants(mid_grad).astype(BF16)

    def sent_all(e, carry):
        @pl.when(e != me)
        def _():
            ship_rows(e).wait_send()
            ship_back(e).wait_send()

        return carry

    lax.fori_loop(0, E, sent_all, 0)

    def left(which, send_at):
        ship(which, store[which].at[0], 0, send_at, twin).wait_send()

    for which in range(2):
        for send_at in (0, 1, 4, 5, 6, 7):
            left(which, send_at)

    @pl.when(inside)
    def _():
        for which in range(2):
            for send_at in (2, 3):
                left(which, send_at)


def moe(mid, grad, gates, ids, w_in, w_out, norm2):
    vmem = pl.BlockSpec(memory_space=pltpu.VMEM)
    anywhere = pl.BlockSpec(memory_space=pl.ANY)
    dma = pltpu.SemaphoreType.DMA
    return pl.pallas_call(
        moe_kernel,
        out_shape=jax.ShapeDtypeStruct((256, 1024), BF16),
        in_specs=[vmem, vmem, vmem, vmem, anywhere, anywhere, vmem],
        out_specs=vmem,
        scratch_shapes=[
            pltpu.VMEM((PIECES, 1024, HID), BF16),
            pltpu.VMEM((PIECES, HID, 1024), BF16),
            pltpu.VMEM((E, 2, C, 1024), BF16),
            pltpu.VMEM((E, 2, C, 1024), BF16),
            pltpu.VMEM((E * C, 1024), F32),
            pltpu.VMEM((E, C, 1024), BF16),
            pltpu.VMEM((E, C, 1024), BF16),
            pltpu.VMEM((256, E * C), BF16),
            dma((2, 8)),
            dma((2, 8)),
            dma((E,)),
            dma((E,)),
            dma((E,)),
            dma((E,)),
        ],
        compiler_params=pltpu.CompilerParams(
            collective_id=0, has_side_effects=True, vmem_limit_bytes=60 * 1024 * 1024
        ),
        name="moe",
    )(mid, grad, gates, ids, w_in, w_out, norm2)


def window_back(window_data, labels):
    tokens_in = window_data.shape[0]
    width = window_data.shape[2]
    head_size = width // HEADS
    scale = head_size ** (-0.5)
    parts = window_data.reshape(tokens_in, 4, HEADS, head_size)
    query = parts[:, 0]
    key_rows = parts[:, 1]
    value_rows = parts[:, 2]
    out_grad = parts[:, 3]
    scores = jnp.einsum("qhd,khd->hqk", query, key_rows, preferred_element_type=F32) * scale
    allowed = (labels[:, None] == labels[None, :])[None, :, :]
    highest = jnp.max(jnp.where(allowed, scores, -1e30), -1, keepdims=True)
    expo = jnp.exp(jnp.where(allowed, scores - highest, -1e30))
    probs = expo / jnp.sum(expo, -1, keepdims=True)
    probs_b = probs.astype(BF16)
    value_grad = jnp.einsum(
        "hqk,qhd->khd", probs_b, out_grad, preferred_element_type=F32
    ).astype(BF16)
    prob_grad = jnp.einsum("qhd,khd->hqk", out_grad, value_rows, preferred_element_type=F32)
    row_total = jnp.sum(probs * prob_grad, -1, keepdims=True)
    score_grad = (probs * (prob_grad - row_total)).astype(BF16)
    query_grad = (
        jnp.einsum("hqk,khd->qhd", score_grad, key_rows, preferred_element_type=F32) * scale
    ).astype(BF16)
    key_grad = (
        jnp.einsum("hqk,qhd->khd", score_grad, query, preferred_element_type=F32) * scale
    ).astype(BF16)
    return jnp.stack((query_grad, key_grad, value_grad), 1).reshape(tokens_in, 3, width)


def shards(
    grad_out, block_in, mid, qkv, gates, expert_ids, w_in, w_out, w_qkv, w_proj, norm1, norm2
):
    window = grad_out.shape[2]
    width = grad_out.shape[4]
    count = window * window
    half = window // 2

    def columns(a):
        return a.reshape(2, half, 2, half, 2).transpose(0, 2, 1, 3, 4).reshape(count, 2)

    mid_grad = moe(
        mid.reshape(count, width),
        grad_out.reshape(count, width),
        columns(gates),
        columns(expert_ids),
        w_in[0],
        w_out[0],
        norm2.reshape(1, width),
    )
    context_grad = jnp.einsum("td,ed->te", mid_grad, w_proj, preferred_element_type=F32).astype(
        BF16
    )
    stacked = jnp.concatenate(
        (qkv.reshape(window, window, 3, width), context_grad.reshape(window, window, 1, width)), 2
    )
    right_part = from_behind(stacked[:, :half], "col", -1)
    widened = jnp.concatenate((stacked[:, half:], right_part), 1)
    lower_part = from_behind(widened[:half], "row", -1)
    shifted = jnp.concatenate((widened[half:], lower_part), 0)
    row_last = lax.axis_index("row") == lax.axis_size("row") - 1
    col_last = lax.axis_index("col") == lax.axis_size("col") - 1
    lower_half = jnp.arange(window) >= half
    row_label = (row_last & lower_half).astype(jnp.int32)
    col_label = (col_last & lower_half).astype(jnp.int32)
    labels = (row_label[:, None] * 2 + col_label[None, :]).reshape(count)
    window_grads = window_back(shifted.reshape(count, 4, width), labels)
    window_grads = jnp.einsum(
        "tc,dc->td", window_grads.reshape(count, 3 * width), w_qkv, preferred_element_type=F32
    )
    window_grads = window_grads.astype(BF16).reshape(window, window, width)
    from_above = from_behind(window_grads[half:], "row", 1)
    widened_grads = jnp.concatenate((from_above, window_grads[:half]), 0)
    from_left = from_behind(widened_grads[:, half:], "col", 1)
    input_normed_grad = jnp.concatenate((from_left, widened_grads[:, :half]), 1)
    input_normed_grad = input_normed_grad.reshape(count, width).astype(F32)
    in_hat, in_inverse = layer_stats(block_in.reshape(count, width))
    result = mid_grad.astype(F32) + norm_back(input_normed_grad, in_hat, in_inverse, norm1)
    return result.astype(BF16).reshape(grad_out.shape)


def solution(mesh):
    return jax.shard_map(
        shards,
        mesh=mesh,
        in_specs=(
            P("row", "col", None, None, None),
            P("row", "col", None, None, None),
            P("row", "col", None, None, None),
            P("row", "col", None, None, None, None),
            P("row", "col", None, None, None),
            P("row", "col", None, None, None),
            P(("row", "col"), None, None),
            P(("row", "col"), None, None),
            P(),
            P(),
            P(),
            P(),
        ),
        out_specs=P("row", "col", None, None, None),
        check_vma=False,
    )
```

```python
import jax
import jax.numpy as jnp
from jax import lax
from jax.experimental import pallas as pl
from jax.experimental.pallas import tpu as pltpu
from jax.sharding import PartitionSpec as P

HEADS = 32
E = 32
C = 32
EPSILON = 1e-05
MESH = pl.DeviceIdType.MESH
F32 = jnp.float32
BF16 = jnp.bfloat16
HID = 512
PIECES = 8


def layer_stats(values):
    floats = values.astype(F32)
    centred = floats - jnp.mean(floats, -1, keepdims=True)
    inverse = lax.rsqrt(jnp.mean(centred * centred, -1, keepdims=True) + EPSILON)
    return (centred * inverse, inverse)


def norm_back(upstream, normal_hat, inverse, gain):
    scaled_up = upstream * gain
    first = jnp.mean(scaled_up, -1, keepdims=True)
    second = jnp.mean(scaled_up * normal_hat, -1, keepdims=True)
    return inverse * (scaled_up - first - normal_hat * second)


def gelu_slope(values):
    return (
        0.5 * (1.0 + lax.erf(values * 0.7071067811865476))
        + values * jnp.exp(-0.5 * values * values) * 0.3989422804014327
    )


def dot(a, b, contract=(1, 0)):
    return lax.dot_general(
        a, b, (((contract[0],), (contract[1],)), ((), ())), preferred_element_type=F32
    )


def to_quadrants(x):
    n = x.shape[-1]
    parts = x.reshape(2, 8, 2, 8, n)
    return jnp.concatenate(
        [parts[a, :, b].reshape(64, n) for a in range(2) for b in range(2)], 0
    )


def from_quadrants(x):
    n = x.shape[-1]
    parts = x.reshape(2, 2, 8, 8, n)
    rows = []
    for a in range(2):
        for i in range(8):
            rows.append(jnp.concatenate([parts[a, 0, i], parts[a, 1, i]], 0))
    return jnp.concatenate(rows, 0)


def position():
    row, col = lax.axis_index("row"), lax.axis_index("col")
    return lax.div(col, 4), lax.div(row, 2), lax.rem(row, 2), lax.rem(col, 4)


def place(x, y, c, z):
    return (2 * y + c, 4 * x + z)


def block_kernel(
    mid_ref,
    grad_ref,
    block_ref,
    qkv_ref,
    gates_ref,
    ids_ref,
    w_in_ref,
    w_out_ref,
    w_qkv_ref,
    w_proj_ref,
    norm1_ref,
    norm2_ref,
    out_ref,
    w_first,
    w_second,
    outgoing,
    arrived,
    total,
    ret_in,
    choice,
    probs,
    window_out,
    window_in,
    context_out,
    context_in,
    heads_grad,
    final_out,
    final_in,
    l_sem,
    h_send,
    h_recv,
    w_send,
    w_recv,
    d_send,
    d_recv,
    r_send,
    r_recv,
):
    x, y, c, z = position()
    pair = lax.div(z, 2)
    u = z + 1 - 2 * lax.rem(z, 2)
    w = 3 - z
    v = 3 - u
    other = 1 - c
    twin = place(x, y, other, z)
    me = 8 * y + 4 * pair + x

    def member(e):
        ex, ey, eb = lax.rem(e, 4), lax.div(e, 8), lax.rem(lax.div(e, 4), 2)
        differs = lax.rem(eb + pair, 2)
        return place(ex, ey, c, z + differs * (3 - 2 * z))

    row, col = lax.axis_index("row"), lax.axis_index("col")
    up, left = lax.rem(row + 7, 8), lax.rem(col + 15, 16)
    down, right = lax.rem(row + 1, 8), lax.rem(col + 1, 16)
    back = ((up, left), (up, col), (row, left))
    ahead = (None, (row, right), (down, col), (down, right))

    barrier = pltpu.get_barrier_semaphore()

    def greet(e, carry):
        @pl.when(e != me)
        def _():
            pl.semaphore_signal(barrier, inc=1, device_id=member(e), device_id_type=MESH)

        return carry

    lax.fori_loop(0, E, greet, 0)
    near = (twin, place(x, y, 0, u), place(x, y, 1, u), place(x, y, other, w))
    for where in near + back + ahead[1:]:
        pl.semaphore_signal(barrier, inc=1, device_id=where, device_id_type=MESH)
    pl.semaphore_wait(barrier, E - 1 + 10)

    def source(which, h):
        if which == 0:
            return w_in_ref.at[:, pl.ds(h * HID, HID)]
        return w_out_ref.at[pl.ds(h * HID, HID), :]

    store = (w_first, w_second)

    def ship(which, src, piece, send_at, where):
        return pltpu.make_async_remote_copy(
            src_ref=src,
            dst_ref=store[which].at[piece],
            send_sem=w_send.at[which, send_at],
            recv_sem=w_recv.at[which, piece],
            device_id=where,
            device_id_type=MESH,
        )

    def local(which, h):
        piece = 2 * z + h
        return pltpu.make_async_copy(
            source(which, h), store[which].at[piece], w_recv.at[which, piece]
        )

    inside = c == pair

    @pl.when(inside)
    def _():
        for h in range(2):
            for which in range(2):
                ship(which, source(which, h), 2 * z + h, h, place(x, y, h, u)).start()
        for h in range(2):
            for which in range(2):
                ship(which, source(which, h), 2 * z + h, 2 + h, twin).start()
                local(which, h).start()

    @pl.when(jnp.logical_not(inside))
    def _():
        for h in range(2):
            for which in range(2):
                ship(which, source(which, h), 2 * z + h, h, place(x, y, h, w)).start()

    norm2 = norm2_ref[...]
    grad = to_quadrants(grad_ref[...].astype(F32))
    mid_hat, mid_inverse = layer_stats(to_quadrants(mid_ref[...].astype(F32)))
    normed = (mid_hat * norm2).astype(BF16)
    gates = gates_ref[...]
    ids = ids_ref[...]
    sent = [(gates[:, k : k + 1] * grad).astype(BF16) for k in range(2)]
    lanes = lax.broadcasted_iota(jnp.int32, (256, E), 1)
    hots = [ids[:, k : k + 1] == lanes for k in range(2)]
    before = (
        lax.broadcasted_iota(jnp.int32, (256, 256), 0)
        > lax.broadcasted_iota(jnp.int32, (256, 256), 1)
    ).astype(BF16)
    hot_f = [h.astype(F32) for h in hots]
    ranks = [dot(before, h.astype(BF16)) for h in hot_f]
    ranks[1] = ranks[1] + jnp.sum(hot_f[0], 0, keepdims=True)
    slots = [
        ids[:, k : k + 1] * C
        + jnp.sum(hot_f[k] * ranks[k], 1, keepdims=True).astype(jnp.int32)
        for k in range(2)
    ]
    wide = lax.broadcasted_iota(jnp.int32, (256, E * C), 1)
    choice[...] = ((slots[0] == wide) | (slots[1] == wide)).astype(BF16)

    def ship_rows(e):
        return pltpu.make_async_remote_copy(
            src_ref=outgoing.at[e],
            dst_ref=arrived.at[me],
            send_sem=d_send.at[e],
            recv_sem=d_recv.at[me],
            device_id=member(e),
            device_id_type=MESH,
        )

    def keep_rows():
        return pltpu.make_async_copy(outgoing.at[me], arrived.at[me], d_recv.at[me])

    narrow = lax.broadcasted_iota(jnp.int32, (256, 256), 1)

    def dispatch(step, carry):
        block = lax.rem(y + step, 4)
        base = block * 256
        picks = [(slots[k] == narrow + base).astype(BF16) for k in range(2)]
        rows_n = dot(picks[0] + picks[1], normed, (0, 0))
        rows_g = dot(picks[0], sent[0], (0, 0)) + dot(picks[1], sent[1], (0, 0))
        outgoing[pl.ds(block * 8, 8), 0] = rows_n.astype(BF16).reshape(8, C, 1024)
        outgoing[pl.ds(block * 8, 8), 1] = rows_g.astype(BF16).reshape(8, C, 1024)

        def send_one(k, carry):
            e = block * 8 + lax.rem(4 * pair + x + k, 8)

            @pl.when(e != me)
            def _():
                ship_rows(e).start()

            @pl.when(e == me)
            def _():
                keep_rows().start()

            return carry

        return lax.fori_loop(0, 8, send_one, carry)

    lax.fori_loop(0, 4, dispatch, 0)
    total[...] = jnp.zeros_like(total)

    def ship_quadrant(stage, src, dst, q, where):
        return pltpu.make_async_remote_copy(
            src_ref=src.at[q],
            dst_ref=dst.at[3 - q],
            send_sem=h_send.at[stage, q],
            recv_sem=h_recv.at[stage, 3 - q],
            device_id=where,
            device_id_type=MESH,
        )

    def quadrant_landed(stage, dst, q):
        pltpu.make_async_copy(dst.at[q], dst.at[q], h_recv.at[stage, q]).wait()

    for part in range(3):
        rows = to_quadrants(qkv_ref[:, part].reshape(256, 1024).astype(F32)).astype(BF16)
        window_out[:, part] = rows.reshape(4, 64, 1024)
        window_in[0, part] = rows[192:]
    for q in range(3):
        ship_quadrant(0, window_out, window_in, q, back[q]).start()
    for q in range(1, 4):
        quadrant_landed(0, window_in, q)

    last_row = (row == 7).astype(jnp.int32)
    last_col = (col == 15).astype(jnp.int32)

    def labels(shape, dim):
        quadrant = lax.div(lax.broadcasted_iota(jnp.int32, shape, dim), 64)
        return lax.div(quadrant, 2) * (2 * last_row) + lax.rem(quadrant, 2) * last_col

    allowed = labels((256, 256), 0) == labels((256, 256), 1)
    shut = jnp.where(allowed, 0.0, -1e30)
    scale = 32**-0.5
    head_of = lax.div(lax.broadcasted_iota(jnp.int32, (256, 128), 1), 32)

    def of_head(h, rows):
        return jnp.where(head_of == h, rows, jnp.zeros_like(rows))

    def window_part(part, lanes_at):
        return window_in[:, part, :, lanes_at].reshape(256, 128)

    def softmax_group(group, carry):
        lanes_at = pl.ds(pl.multiple_of(group * 128, 128), 128)
        query, key = window_part(0, lanes_at), window_part(1, lanes_at)
        for h in range(4):
            scores = dot(of_head(h, key), query, (1, 1)) * scale + shut
            expo = jnp.exp(scores - jnp.max(scores, 0, keepdims=True))
            probs[4 * group + h] = (expo * (1.0 / jnp.sum(expo, 0, keepdims=True))).astype(BF16)
        return carry

    lax.fori_loop(0, HEADS // 4, softmax_group, 0)

    def landed(which, piece):
        pltpu.make_async_copy(
            store[which].at[piece], store[which].at[piece], w_recv.at[which, piece]
        ).wait()

    def pass_on(piece, send_at, targets):
        for which in range(2):
            landed(which, piece)
            for n, where in enumerate(targets):
                ship(which, store[which].at[piece], piece, send_at + n, where).start()

    def product(piece, rows, begin):
        count = rows // C
        at = pl.ds(begin, count)
        normed_rows = arrived[at, 0].reshape(rows, 1024)
        grad_rows = arrived[at, 1].reshape(rows, 1024)
        first, second = w_first[piece], w_second[piece]
        pre = dot(normed_rows, first)
        act_grad = dot(grad_rows, second, (1, 1))
        pre_grad = (act_grad * gelu_slope(pre)).astype(BF16)
        return dot(pre_grad, first, (1, 1))

    def whole(piece, rows=512):
        def one(step, carry):
            at = pl.ds(pl.multiple_of(step * rows, rows), rows)
            total[at] = total[at] + product(piece, rows, step * (rows // C))
            return carry

        lax.fori_loop(0, 1024 // rows, one, 0)

    pass_on(2 * w + c, 4, (place(x, y, c, u), twin))
    pass_on(2 * u + c, 6, (twin,))

    def rows_landed(m, carry):
        pltpu.make_async_copy(arrived.at[m], arrived.at[m], d_recv.at[m]).wait()
        return carry

    lax.fori_loop(0, E, rows_landed, 0)
    for h in range(2):
        for which in range(2):
            landed(which, 2 * z + h)
        whole(2 * z + h)
    whole(2 * u + c)
    whole(2 * w + c)
    for which in range(2):
        landed(which, 2 * u + other)
    whole(2 * u + other)
    for which in range(2):
        landed(which, 2 * w + other)
    whole(2 * w + other)
    pass_on(2 * v + c, 7, (twin,))
    whole(2 * v + c)
    for which in range(2):
        landed(which, 2 * v + other)

    def rows_gone(e, carry):
        @pl.when(e != me)
        def _():
            ship_rows(e).wait_send()

        return carry

    lax.fori_loop(0, E, rows_gone, 0)

    def ship_back(m):
        return pltpu.make_async_remote_copy(
            src_ref=outgoing.at[m, 0],
            dst_ref=ret_in.at[me],
            send_sem=r_send.at[m],
            recv_sem=r_recv.at[me],
            device_id=member(m),
            device_id_type=MESH,
        )

    def last(step, carry):
        block = lax.rem(y + step, 4)
        at = pl.ds(pl.multiple_of(block * 256, 256), 256)
        done = total[at] + product(2 * v + other, 256, block * 8)
        outgoing[pl.ds(block * 8, 8), 0] = done.astype(BF16).reshape(8, C, 1024)

        def send_one(k, carry):
            m = block * 8 + lax.rem(4 * pair + x + k, 8)

            @pl.when(m != me)
            def _():
                ship_back(m).start()

            @pl.when(m == me)
            def _():
                pltpu.make_async_copy(
                    outgoing.at[me, 0], ret_in.at[me], r_recv.at[me]
                ).start()

            return carry

        return lax.fori_loop(0, 8, send_one, carry)

    lax.fori_loop(0, 4, last, 0)

    def gone(which, send_at):
        ship(which, store[which].at[0], 0, send_at, twin).wait_send()

    for which in range(2):
        for send_at in (0, 1, 4, 5, 6, 7):
            gone(which, send_at)

    @pl.when(inside)
    def _():
        for which in range(2):
            for send_at in (2, 3):
                gone(which, send_at)

    loads = [
        pltpu.make_async_copy(
            w_proj_ref.at[pl.ds(k * HID, HID), :], w_second.at[k], l_sem.at[k]
        )
        for k in range(2)
    ] + [
        pltpu.make_async_copy(
            w_qkv_ref.at[:, pl.ds(k * HID, HID)], w_first.at[k], l_sem.at[2 + k]
        )
        for k in range(6)
    ]
    for load in loads:
        load.start()

    def back_landed(m, carry):
        pltpu.make_async_copy(ret_in.at[m], ret_in.at[m], r_recv.at[m]).wait()
        return carry

    lax.fori_loop(0, E, back_landed, 0)
    normed_grad = dot(choice[...], ret_in[...].reshape(E * C, 1024))
    mid_grad = grad + norm_back(normed_grad, mid_hat, mid_inverse, norm2)
    mid_grad = mid_grad.astype(BF16)

    for load in loads:
        load.wait()
    context_grad = jnp.concatenate(
        [dot(mid_grad, w_second[k], (1, 1)).astype(BF16) for k in range(2)], 1
    )
    context_out[...] = context_grad.reshape(4, 64, 1024)
    for q in range(3):
        ship_quadrant(1, context_out, context_in, q, back[q]).start()
    context_in[0] = context_grad[192:]
    in_hat, in_inverse = layer_stats(to_quadrants(block_ref[...].astype(F32)))
    for q in range(1, 4):
        quadrant_landed(1, context_in, q)

    def heads_back(group, carry):
        begin = pl.multiple_of(group * 128, 128)
        lanes_at = pl.ds(begin, 128)
        query, key, value = (window_part(part, lanes_at) for part in range(3))
        out_grad = context_in[:, :, lanes_at].reshape(256, 128)
        sums = [jnp.zeros((256, 128), F32)] * 3
        for h in range(4):
            prob = probs[4 * group + h]
            prob_f = prob.astype(F32)
            prob_grad = dot(of_head(h, value), out_grad, (1, 1))
            row_total = jnp.sum(prob_f * prob_grad, 0, keepdims=True)
            score_grad = (prob_f * (prob_grad - row_total)).astype(BF16)
            sums = [
                sums[0] + dot(score_grad, of_head(h, key), (0, 0)),
                sums[1] + dot(score_grad, of_head(h, query)),
                sums[2] + dot(prob, of_head(h, out_grad)),
            ]
        for part, factor in enumerate((scale, scale, 1.0)):
            at = pl.ds(pl.multiple_of(part * 1024 + begin, 128), 128)
            heads_grad[:, at] = (sums[part] * factor).astype(BF16)
        return carry

    lax.fori_loop(0, HEADS // 4, heads_back, 0)

    def project(step, carry):
        at = pl.ds(pl.multiple_of(step * 256, 256), 256)
        part = sum(
            dot(heads_grad[:, k * HID : (k + 1) * HID], w_first[k, at, :], (1, 1))
            for k in range(6)
        )
        final_out[:, :, at] = part.astype(BF16).reshape(4, 64, 256)
        return carry

    lax.fori_loop(0, 4, project, 0)
    for q in range(1, 4):
        ship_quadrant(2, final_out, final_in, q, ahead[q]).start()
    final_in[3] = final_out[0]
    for q in range(3):
        quadrant_landed(2, final_in, q)
    upstream = final_in[...].reshape(256, 1024).astype(F32)
    result = mid_grad.astype(F32) + norm_back(upstream, in_hat, in_inverse, norm1_ref[...])
    out_ref[...] = from_quadrants(result).astype(BF16)

    def sent_all(e, carry):
        @pl.when(e != me)
        def _():
            ship_back(e).wait_send()

        return carry

    lax.fori_loop(0, E, sent_all, 0)
    for q in range(3):
        ship_quadrant(0, window_out, window_in, q, back[q]).wait_send()
        ship_quadrant(1, context_out, context_in, q, back[q]).wait_send()
        ship_quadrant(2, final_out, final_in, q + 1, ahead[q + 1]).wait_send()


def block(mid, grad, block_in, qkv, gates, ids, w_in, w_out, w_qkv, w_proj, norm1, norm2):
    vmem = pl.BlockSpec(memory_space=pltpu.VMEM)
    anywhere = pl.BlockSpec(memory_space=pl.ANY)
    dma = pltpu.SemaphoreType.DMA
    return pl.pallas_call(
        block_kernel,
        out_shape=jax.ShapeDtypeStruct((256, 1024), BF16),
        in_specs=[vmem] * 6 + [anywhere] * 4 + [vmem] * 2,
        out_specs=vmem,
        scratch_shapes=[
            pltpu.VMEM((PIECES, 1024, HID), BF16),
            pltpu.VMEM((PIECES, HID, 1024), BF16),
            pltpu.VMEM((E, 2, C, 1024), BF16),
            pltpu.VMEM((E, 2, C, 1024), BF16),
            pltpu.VMEM((E * C, 1024), F32),
            pltpu.VMEM((E, C, 1024), BF16),
            pltpu.VMEM((256, E * C), BF16),
            pltpu.VMEM((HEADS, 256, 256), BF16),
            pltpu.VMEM((4, 3, 64, 1024), BF16),
            pltpu.VMEM((4, 3, 64, 1024), BF16),
            pltpu.VMEM((4, 64, 1024), BF16),
            pltpu.VMEM((4, 64, 1024), BF16),
            pltpu.VMEM((256, 3072), BF16),
            pltpu.VMEM((4, 64, 1024), BF16),
            pltpu.VMEM((4, 64, 1024), BF16),
            dma((8,)),
            dma((3, 4)),
            dma((3, 4)),
            dma((2, 8)),
            dma((2, 8)),
            dma((E,)),
            dma((E,)),
            dma((E,)),
            dma((E,)),
        ],
        compiler_params=pltpu.CompilerParams(
            collective_id=0, has_side_effects=True, vmem_limit_bytes=62 * 1024 * 1024
        ),
        name="block",
    )(mid, grad, block_in, qkv, gates, ids, w_in, w_out, w_qkv, w_proj, norm1, norm2)


def shards(
    grad_out, block_in, mid, qkv, gates, expert_ids, w_in, w_out, w_qkv, w_proj, norm1, norm2
):
    window = grad_out.shape[2]
    width = grad_out.shape[4]
    count = window * window
    half = window // 2

    def columns(a):
        return a.reshape(2, half, 2, half, 2).transpose(0, 2, 1, 3, 4).reshape(count, 2)

    result = block(
        mid.reshape(count, width),
        grad_out.reshape(count, width),
        block_in.reshape(count, width),
        qkv.reshape(window, window, 3, width).transpose(0, 2, 1, 3),
        columns(gates),
        columns(expert_ids),
        w_in[0],
        w_out[0],
        w_qkv,
        w_proj,
        norm1.reshape(1, width),
        norm2.reshape(1, width),
    )
    return result.reshape(grad_out.shape)


def solution(mesh):
    return jax.shard_map(
        shards,
        mesh=mesh,
        in_specs=(
            P("row", "col", None, None, None),
            P("row", "col", None, None, None),
            P("row", "col", None, None, None),
            P("row", "col", None, None, None, None),
            P("row", "col", None, None, None),
            P("row", "col", None, None, None),
            P(("row", "col"), None, None),
            P(("row", "col"), None, None),
            P(),
            P(),
            P(),
            P(),
        ),
        out_specs=P("row", "col", None, None, None),
        check_vma=False,
    )
```

```python
import jax
import jax.numpy as jnp
from jax import lax
from jax.experimental import pallas as pl
from jax.experimental.pallas import tpu as pltpu
from jax.sharding import PartitionSpec as P

HEADS = 32
E = 32
C = 32
EPSILON = 1e-05
MESH = pl.DeviceIdType.MESH
F32 = jnp.float32
BF16 = jnp.bfloat16
HID = 512
PIECES = 8


def layer_stats(values):
    floats = values.astype(F32)
    centred = floats - jnp.mean(floats, -1, keepdims=True)
    inverse = lax.rsqrt(jnp.mean(centred * centred, -1, keepdims=True) + EPSILON)
    return (centred * inverse, inverse)


def norm_back(upstream, normal_hat, inverse, gain):
    scaled_up = upstream * gain
    first = jnp.mean(scaled_up, -1, keepdims=True)
    second = jnp.mean(scaled_up * normal_hat, -1, keepdims=True)
    return inverse * (scaled_up - first - normal_hat * second)


def gelu_slope(values):
    return (
        0.5 * (1.0 + lax.erf(values * 0.7071067811865476))
        + values * jnp.exp(-0.5 * values * values) * 0.3989422804014327
    )


def dot(a, b, contract=(1, 0)):
    return lax.dot_general(
        a, b, (((contract[0],), (contract[1],)), ((), ())), preferred_element_type=F32
    )


def to_quadrants(x):
    n = x.shape[-1]
    parts = x.reshape(2, 8, 2, 8, n)
    return jnp.concatenate(
        [parts[a, :, b].reshape(64, n) for a in range(2) for b in range(2)], 0
    )


def from_quadrants(x):
    n = x.shape[-1]
    parts = x.reshape(2, 2, 8, 8, n)
    rows = []
    for a in range(2):
        for i in range(8):
            rows.append(jnp.concatenate([parts[a, 0, i], parts[a, 1, i]], 0))
    return jnp.concatenate(rows, 0)


def position():
    row, col = lax.axis_index("row"), lax.axis_index("col")
    return lax.div(col, 4), lax.div(row, 2), lax.rem(row, 2), lax.rem(col, 4)


def place(x, y, c, z):
    return (2 * y + c, 4 * x + z)


def block_kernel(
    mid_ref,
    grad_ref,
    block_ref,
    qkv_ref,
    routes_ref,
    w_in_ref,
    w_out_ref,
    w_qkv_ref,
    w_proj_ref,
    norm1_ref,
    norm2_ref,
    out_ref,
    w_first,
    w_second,
    mate_mid,
    mate_grad,
    mate_routes,
    outgoing,
    arrived,
    total,
    ret_in,
    choice,
    probs,
    window_out,
    window_in,
    context_out,
    context_in,
    heads_grad,
    final_out,
    final_in,
    l_sem,
    h_send,
    h_recv,
    m_send,
    m_recv,
    w_send,
    w_recv,
    d_send,
    d_recv,
    r_send,
    r_recv,
):
    x, y, c, z = position()
    pair = lax.div(z, 2)
    u = z + 1 - 2 * lax.rem(z, 2)
    w = 3 - z
    v = 3 - u
    other = 1 - c
    twin = place(x, y, other, z)
    me = 8 * y + 4 * pair + x
    mate = 8 * y + 4 * (1 - pair) + x

    def member(e):
        ex, ey, eb = lax.rem(e, 4), lax.div(e, 8), lax.rem(lax.div(e, 4), 2)
        differs = lax.rem(eb + pair, 2)
        return place(ex, ey, c, z + differs * (3 - 2 * z))

    row, col = lax.axis_index("row"), lax.axis_index("col")
    up, left = lax.rem(row + 7, 8), lax.rem(col + 15, 16)
    down, right = lax.rem(row + 1, 8), lax.rem(col + 1, 16)
    back = ((up, left), (up, col), (row, left))
    ahead = (None, (row, right), (down, col), (down, right))

    barrier = pltpu.get_barrier_semaphore()

    def greet(e, carry):
        @pl.when(e != me)
        def _():
            pl.semaphore_signal(barrier, inc=1, device_id=member(e), device_id_type=MESH)

        return carry

    lax.fori_loop(0, E, greet, 0)
    near = (twin, place(x, y, 0, u), place(x, y, 1, u), place(x, y, other, w))
    for where in near + back + ahead[1:]:
        pl.semaphore_signal(barrier, inc=1, device_id=where, device_id_type=MESH)
    pl.semaphore_wait(barrier, E - 1 + 10)

    def source(which, h):
        if which == 0:
            return w_in_ref.at[:, pl.ds(h * HID, HID)]
        return w_out_ref.at[pl.ds(h * HID, HID), :]

    store = (w_first, w_second)

    def ship(which, src, piece, send_at, where):
        return pltpu.make_async_remote_copy(
            src_ref=src,
            dst_ref=store[which].at[piece],
            send_sem=w_send.at[which, send_at],
            recv_sem=w_recv.at[which, piece],
            device_id=where,
            device_id_type=MESH,
        )

    def local(which, h):
        piece = 2 * z + h
        return pltpu.make_async_copy(
            source(which, h), store[which].at[piece], w_recv.at[which, piece]
        )

    inside = c == pair
    outside = jnp.logical_not(inside)

    tile = (
        (mid_ref, mate_mid),
        (grad_ref, mate_grad),
        (routes_ref, mate_routes),
    )

    def ship_tile(n):
        return pltpu.make_async_remote_copy(
            src_ref=tile[n][0],
            dst_ref=tile[n][1],
            send_sem=m_send.at[n],
            recv_sem=m_recv.at[n],
            device_id=place(x, y, c, w),
            device_id_type=MESH,
        )

    for n in range(3):
        ship_tile(n).start()

    @pl.when(inside)
    def _():
        for h in range(2):
            for which in range(2):
                ship(which, source(which, h), 2 * z + h, h, place(x, y, h, u)).start()
        for h in range(2):
            for which in range(2):
                ship(which, source(which, h), 2 * z + h, 2 + h, twin).start()
                local(which, h).start()

    def cross(which, h):
        return ship(which, source(which, h), 2 * z + h, h, place(x, y, h, w))

    norm2 = norm2_ref[...]

    def prepare(mid_rows, grad_rows, routes):
        grad = to_quadrants(grad_rows.astype(F32))
        mid_hat, mid_inverse = layer_stats(to_quadrants(mid_rows.astype(F32)))
        normed = (mid_hat * norm2).astype(BF16)
        ids = routes[:, 2:4].astype(jnp.int32)
        sent = [(routes[:, k : k + 1] * grad).astype(BF16) for k in range(2)]
        lanes = lax.broadcasted_iota(jnp.int32, (256, E), 1)
        hots = [(ids[:, k : k + 1] == lanes).astype(F32) for k in range(2)]
        before = (
            lax.broadcasted_iota(jnp.int32, (256, 256), 0)
            > lax.broadcasted_iota(jnp.int32, (256, 256), 1)
        ).astype(BF16)
        ranks = [dot(before, h.astype(BF16)) for h in hots]
        ranks[1] = ranks[1] + jnp.sum(hots[0], 0, keepdims=True)
        slots = [
            ids[:, k : k + 1] * C
            + jnp.sum(hots[k] * ranks[k], 1, keepdims=True).astype(jnp.int32)
            for k in range(2)
        ]
        return grad, mid_hat, mid_inverse, normed, sent, slots

    def ship_rows(at, origin, ex, ey):
        return pltpu.make_async_remote_copy(
            src_ref=outgoing.at[at],
            dst_ref=arrived.at[origin],
            send_sem=d_send.at[at],
            recv_sem=d_recv.at[origin],
            device_id=place(ex, ey, c, z),
            device_id_type=MESH,
        )

    narrow = lax.broadcasted_iota(jnp.int32, (256, 128), 1)

    def dispatch(normed, sent, slots, bit, origin):
        def one(step, carry):
            ey = lax.rem(y + step, 4)
            base = (8 * ey + 4 * pair) * C
            picks = [(slots[k] == narrow + base).astype(BF16) for k in range(2)]
            rows_n = dot(picks[0] + picks[1], normed, (0, 0))
            rows_g = dot(picks[0], sent[0], (0, 0)) + dot(picks[1], sent[1], (0, 0))
            begin = 8 * ey + 4 * bit
            outgoing[pl.ds(begin, 4), 0] = rows_n.astype(BF16).reshape(4, C, 1024)
            outgoing[pl.ds(begin, 4), 1] = rows_g.astype(BF16).reshape(4, C, 1024)

            def send_one(k, carry):
                ex = lax.rem(x + k, 4)
                at = begin + ex
                here = at == 8 * y + 4 * bit + x

                @pl.when(jnp.logical_not(here))
                def _():
                    ship_rows(at, origin, ex, ey).start()

                @pl.when(here)
                def _():
                    pltpu.make_async_copy(
                        outgoing.at[at], arrived.at[origin], d_recv.at[origin]
                    ).start()

                return carry

            return lax.fori_loop(0, 4, send_one, carry)

        lax.fori_loop(0, 4, one, 0)

    grad, mid_hat, mid_inverse, normed, sent, slots = prepare(
        mid_ref[...], grad_ref[...], routes_ref[...]
    )
    wide = lax.broadcasted_iota(jnp.int32, (256, E * C), 1)
    choice[...] = ((slots[0] == wide) | (slots[1] == wide)).astype(BF16)
    dispatch(normed, sent, slots, pair, me)
    total[...] = jnp.zeros_like(total)

    def ship_quadrant(stage, src, dst, q, where):
        return pltpu.make_async_remote_copy(
            src_ref=src.at[q],
            dst_ref=dst.at[3 - q],
            send_sem=h_send.at[stage, q],
            recv_sem=h_recv.at[stage, 3 - q],
            device_id=where,
            device_id_type=MESH,
        )

    def quadrant_landed(stage, dst, q):
        pltpu.make_async_copy(dst.at[q], dst.at[q], h_recv.at[stage, q]).wait()

    for part in range(3):
        rows = to_quadrants(qkv_ref[:, part].reshape(256, 1024).astype(F32)).astype(BF16)
        window_out[:, part] = rows.reshape(4, 64, 1024)
        window_in[0, part] = rows[192:]
    for q in range(3):
        ship_quadrant(0, window_out, window_in, q, back[q]).start()
    for n in range(3):
        ship_tile(n).wait_send()

    @pl.when(outside)
    def _():
        for h in range(2):
            cross(0, h).start()

    for n in range(3):
        pltpu.make_async_copy(tile[n][1], tile[n][1], m_recv.at[n]).wait()
    _, _, _, normed_m, sent_m, slots_m = prepare(
        mate_mid[...], mate_grad[...], mate_routes[...]
    )
    dispatch(normed_m, sent_m, slots_m, 1 - pair, mate)

    for q in range(1, 4):
        quadrant_landed(0, window_in, q)

    last_row = (row == 7).astype(jnp.int32)
    last_col = (col == 15).astype(jnp.int32)

    def labels(shape, dim):
        quadrant = lax.div(lax.broadcasted_iota(jnp.int32, shape, dim), 64)
        return lax.div(quadrant, 2) * (2 * last_row) + lax.rem(quadrant, 2) * last_col

    allowed = labels((256, 256), 0) == labels((256, 256), 1)
    shut = jnp.where(allowed, 0.0, -1e30)
    scale = 32**-0.5
    head_of = lax.div(lax.broadcasted_iota(jnp.int32, (256, 128), 1), 32)

    def of_head(h, rows):
        return jnp.where(head_of == h, rows, jnp.zeros_like(rows))

    def window_part(part, lanes_at):
        return window_in[:, part, :, lanes_at].reshape(256, 128)

    def softmax_group(group, carry):
        lanes_at = pl.ds(pl.multiple_of(group * 128, 128), 128)
        query, key = window_part(0, lanes_at), window_part(1, lanes_at)
        for h in range(4):
            scores = dot(of_head(h, key), query, (1, 1)) * scale + shut
            expo = jnp.exp(scores - jnp.max(scores, 0, keepdims=True))
            probs[4 * group + h] = (expo * (1.0 / jnp.sum(expo, 0, keepdims=True))).astype(BF16)
        return carry

    lax.fori_loop(0, HEADS // 4, softmax_group, 0)

    def landed(which, piece):
        pltpu.make_async_copy(
            store[which].at[piece], store[which].at[piece], w_recv.at[which, piece]
        ).wait()

    def pass_on(which, piece, send_at, targets):
        landed(which, piece)
        for n, where in enumerate(targets):
            ship(which, store[which].at[piece], piece, send_at + n, where).start()

    def product(piece, rows, begin):
        count = rows // C
        at = pl.ds(begin, count)
        normed_rows = arrived[at, 0].reshape(rows, 1024)
        grad_rows = arrived[at, 1].reshape(rows, 1024)
        first, second = w_first[piece], w_second[piece]
        pre = dot(normed_rows, first)
        act_grad = dot(grad_rows, second, (1, 1))
        pre_grad = (act_grad * gelu_slope(pre)).astype(BF16)
        return dot(pre_grad, first, (1, 1))

    def whole(piece, rows=512):
        def one(step, carry):
            at = pl.ds(pl.multiple_of(step * rows, rows), rows)
            total[at] = total[at] + product(piece, rows, step * (rows // C))
            return carry

        lax.fori_loop(0, 1024 // rows, one, 0)

    @pl.when(outside)
    def _():
        for h in range(2):
            cross(0, h).wait_send()
            cross(1, h).start()

    onward = (place(x, y, c, u), twin)
    pass_on(0, 2 * w + c, 4, onward)
    for which in range(2):
        pass_on(which, 2 * u + c, 6, (twin,))

    def rows_landed(m, carry):
        pltpu.make_async_copy(arrived.at[m], arrived.at[m], d_recv.at[m]).wait()
        return carry

    lax.fori_loop(0, E, rows_landed, 0)
    for which in range(2):
        landed(which, 2 * z)
    whole(2 * z)
    pass_on(1, 2 * w + c, 4, onward)
    for which in range(2):
        landed(which, 2 * z + 1)
    whole(2 * z + 1)
    whole(2 * u + c)
    whole(2 * w + c)
    pass_on(0, 2 * v + c, 7, (twin,))
    for which in range(2):
        landed(which, 2 * u + other)
    whole(2 * u + other)
    for which in range(2):
        landed(which, 2 * w + other)
    whole(2 * w + other)
    pass_on(1, 2 * v + c, 7, (twin,))
    whole(2 * v + c)
    for which in range(2):
        landed(which, 2 * v + other)

    def rows_gone(at, carry):
        @pl.when((at != me) & (at != mate))
        def _():
            ship_rows(at, me, x, y).wait_send()

        return carry

    lax.fori_loop(0, E, rows_gone, 0)

    def ship_back(m):
        return pltpu.make_async_remote_copy(
            src_ref=outgoing.at[m, 0],
            dst_ref=ret_in.at[me],
            send_sem=r_send.at[m],
            recv_sem=r_recv.at[me],
            device_id=member(m),
            device_id_type=MESH,
        )

    def last(step, carry):
        block = lax.rem(y + step, 4)
        at = pl.ds(pl.multiple_of(block * 256, 256), 256)
        done = total[at] + product(2 * v + other, 256, block * 8)
        outgoing[pl.ds(block * 8, 8), 0] = done.astype(BF16).reshape(8, C, 1024)

        def send_one(k, carry):
            m = block * 8 + lax.rem(4 * pair + x + k, 8)

            @pl.when(m != me)
            def _():
                ship_back(m).start()

            @pl.when(m == me)
            def _():
                pltpu.make_async_copy(
                    outgoing.at[me, 0], ret_in.at[me], r_recv.at[me]
                ).start()

            return carry

        return lax.fori_loop(0, 8, send_one, carry)

    lax.fori_loop(0, 4, last, 0)

    def gone(which, send_at):
        ship(which, store[which].at[0], 0, send_at, twin).wait_send()

    for which in range(2):
        for send_at in (4, 5, 6, 7):
            gone(which, send_at)

    @pl.when(inside)
    def _():
        for which in range(2):
            for send_at in range(4):
                gone(which, send_at)

    @pl.when(outside)
    def _():
        for send_at in range(2):
            gone(1, send_at)

    loads = [
        pltpu.make_async_copy(
            w_proj_ref.at[pl.ds(k * HID, HID), :], w_second.at[k], l_sem.at[k]
        )
        for k in range(2)
    ] + [
        pltpu.make_async_copy(
            w_qkv_ref.at[:, pl.ds(k * HID, HID)], w_first.at[k], l_sem.at[2 + k]
        )
        for k in range(6)
    ]
    for load in loads:
        load.start()

    def back_landed(m, carry):
        pltpu.make_async_copy(ret_in.at[m], ret_in.at[m], r_recv.at[m]).wait()
        return carry

    lax.fori_loop(0, E, back_landed, 0)
    normed_grad = dot(choice[...], ret_in[...].reshape(E * C, 1024))
    mid_grad = grad + norm_back(normed_grad, mid_hat, mid_inverse, norm2)
    mid_grad = mid_grad.astype(BF16)

    for load in loads:
        load.wait()
    context_grad = jnp.concatenate(
        [dot(mid_grad, w_second[k], (1, 1)).astype(BF16) for k in range(2)], 1
    )
    context_out[...] = context_grad.reshape(4, 64, 1024)
    for q in range(3):
        ship_quadrant(1, context_out, context_in, q, back[q]).start()
    context_in[0] = context_grad[192:]
    in_hat, in_inverse = layer_stats(to_quadrants(block_ref[...].astype(F32)))
    for q in range(1, 4):
        quadrant_landed(1, context_in, q)

    def heads_back(group, carry):
        begin = pl.multiple_of(group * 128, 128)
        lanes_at = pl.ds(begin, 128)
        query, key, value = (window_part(part, lanes_at) for part in range(3))
        out_grad = context_in[:, :, lanes_at].reshape(256, 128)
        sums = [jnp.zeros((256, 128), F32)] * 3
        for h in range(4):
            prob = probs[4 * group + h]
            prob_f = prob.astype(F32)
            prob_grad = dot(of_head(h, value), out_grad, (1, 1))
            row_total = jnp.sum(prob_f * prob_grad, 0, keepdims=True)
            score_grad = (prob_f * (prob_grad - row_total)).astype(BF16)
            sums = [
                sums[0] + dot(score_grad, of_head(h, key), (0, 0)),
                sums[1] + dot(score_grad, of_head(h, query)),
                sums[2] + dot(prob, of_head(h, out_grad)),
            ]
        for part, factor in enumerate((scale, scale, 1.0)):
            at = pl.ds(pl.multiple_of(part * 1024 + begin, 128), 128)
            heads_grad[:, at] = (sums[part] * factor).astype(BF16)
        return carry

    lax.fori_loop(0, HEADS // 4, heads_back, 0)

    def project(step, carry):
        at = pl.ds(pl.multiple_of(step * 256, 256), 256)
        part = sum(
            dot(heads_grad[:, k * HID : (k + 1) * HID], w_first[k, at, :], (1, 1))
            for k in range(6)
        )
        final_out[:, :, at] = part.astype(BF16).reshape(4, 64, 256)
        return carry

    lax.fori_loop(0, 4, project, 0)
    for q in range(1, 4):
        ship_quadrant(2, final_out, final_in, q, ahead[q]).start()
    final_in[3] = final_out[0]
    for q in range(3):
        quadrant_landed(2, final_in, q)
    upstream = final_in[...].reshape(256, 1024).astype(F32)
    result = mid_grad.astype(F32) + norm_back(upstream, in_hat, in_inverse, norm1_ref[...])
    out_ref[...] = from_quadrants(result).astype(BF16)

    def sent_all(e, carry):
        @pl.when(e != me)
        def _():
            ship_back(e).wait_send()

        return carry

    lax.fori_loop(0, E, sent_all, 0)
    for q in range(3):
        ship_quadrant(0, window_out, window_in, q, back[q]).wait_send()
        ship_quadrant(1, context_out, context_in, q, back[q]).wait_send()
        ship_quadrant(2, final_out, final_in, q + 1, ahead[q + 1]).wait_send()


def block(mid, grad, block_in, qkv, routes, w_in, w_out, w_qkv, w_proj, norm1, norm2):
    vmem = pl.BlockSpec(memory_space=pltpu.VMEM)
    anywhere = pl.BlockSpec(memory_space=pl.ANY)
    dma = pltpu.SemaphoreType.DMA
    return pl.pallas_call(
        block_kernel,
        out_shape=jax.ShapeDtypeStruct((256, 1024), BF16),
        in_specs=[vmem] * 5 + [anywhere] * 4 + [vmem] * 2,
        out_specs=vmem,
        scratch_shapes=[
            pltpu.VMEM((PIECES, 1024, HID), BF16),
            pltpu.VMEM((PIECES, HID, 1024), BF16),
            pltpu.VMEM((256, 1024), BF16),
            pltpu.VMEM((256, 1024), BF16),
            pltpu.VMEM((256, 128), F32),
            pltpu.VMEM((E, 2, C, 1024), BF16),
            pltpu.VMEM((E, 2, C, 1024), BF16),
            pltpu.VMEM((E * C, 1024), F32),
            pltpu.VMEM((E, C, 1024), BF16),
            pltpu.VMEM((256, E * C), BF16),
            pltpu.VMEM((HEADS, 256, 256), BF16),
            pltpu.VMEM((4, 3, 64, 1024), BF16),
            pltpu.VMEM((4, 3, 64, 1024), BF16),
            pltpu.VMEM((4, 64, 1024), BF16),
            pltpu.VMEM((4, 64, 1024), BF16),
            pltpu.VMEM((256, 3072), BF16),
            pltpu.VMEM((4, 64, 1024), BF16),
            pltpu.VMEM((4, 64, 1024), BF16),
            dma((8,)),
            dma((3, 4)),
            dma((3, 4)),
            dma((3,)),
            dma((3,)),
            dma((2, 8)),
            dma((2, 8)),
            dma((E,)),
            dma((E,)),
            dma((E,)),
            dma((E,)),
        ],
        compiler_params=pltpu.CompilerParams(
            collective_id=0, has_side_effects=True, vmem_limit_bytes=62 * 1024 * 1024
        ),
        name="block",
    )(mid, grad, block_in, qkv, routes, w_in, w_out, w_qkv, w_proj, norm1, norm2)


def shards(
    grad_out, block_in, mid, qkv, gates, expert_ids, w_in, w_out, w_qkv, w_proj, norm1, norm2
):
    window = grad_out.shape[2]
    width = grad_out.shape[4]
    count = window * window
    half = window // 2

    routes = jnp.concatenate((gates, expert_ids.astype(F32)), -1)
    routes = routes.reshape(2, half, 2, half, 4).transpose(0, 2, 1, 3, 4).reshape(count, 4)
    routes = jnp.pad(routes, ((0, 0), (0, 124)))
    result = block(
        mid.reshape(count, width),
        grad_out.reshape(count, width),
        block_in.reshape(count, width),
        qkv.reshape(window, window, 3, width).transpose(0, 2, 1, 3),
        routes,
        w_in[0],
        w_out[0],
        w_qkv,
        w_proj,
        norm1.reshape(1, width),
        norm2.reshape(1, width),
    )
    return result.reshape(grad_out.shape)


def solution(mesh):
    return jax.shard_map(
        shards,
        mesh=mesh,
        in_specs=(
            P("row", "col", None, None, None),
            P("row", "col", None, None, None),
            P("row", "col", None, None, None),
            P("row", "col", None, None, None, None),
            P("row", "col", None, None, None),
            P("row", "col", None, None, None),
            P(("row", "col"), None, None),
            P(("row", "col"), None, None),
            P(),
            P(),
            P(),
            P(),
        ),
        out_specs=P("row", "col", None, None, None),
        check_vma=False,
    )
```

```python
import jax
import jax.numpy as jnp
from jax import lax
from jax.experimental import pallas as pl
from jax.experimental.pallas import tpu as pltpu
from jax.sharding import PartitionSpec as P

HEADS = 32
E = 32
C = 32
EPSILON = 1e-05
MESH = pl.DeviceIdType.MESH
F32 = jnp.float32
BF16 = jnp.bfloat16
HID = 512
PIECES = 8


def layer_stats(values):
    floats = values.astype(F32)
    centred = floats - jnp.mean(floats, -1, keepdims=True)
    inverse = lax.rsqrt(jnp.mean(centred * centred, -1, keepdims=True) + EPSILON)
    return (centred * inverse, inverse)


def norm_back(upstream, normal_hat, inverse, gain):
    scaled_up = upstream * gain
    first = jnp.mean(scaled_up, -1, keepdims=True)
    second = jnp.mean(scaled_up * normal_hat, -1, keepdims=True)
    return inverse * (scaled_up - first - normal_hat * second)


def gelu_slope(values):
    return (
        0.5 * (1.0 + lax.erf(values * 0.7071067811865476))
        + values * jnp.exp(-0.5 * values * values) * 0.3989422804014327
    )


def dot(a, b, contract=(1, 0)):
    return lax.dot_general(
        a, b, (((contract[0],), (contract[1],)), ((), ())), preferred_element_type=F32
    )


def to_quadrants(x):
    n = x.shape[-1]
    parts = x.reshape(2, 8, 2, 8, n)
    return jnp.concatenate(
        [parts[a, :, b].reshape(64, n) for a in range(2) for b in range(2)], 0
    )


def from_quadrants(x):
    n = x.shape[-1]
    parts = x.reshape(2, 2, 8, 8, n)
    rows = []
    for a in range(2):
        for i in range(8):
            rows.append(jnp.concatenate([parts[a, 0, i], parts[a, 1, i]], 0))
    return jnp.concatenate(rows, 0)


def position():
    row, col = lax.axis_index("row"), lax.axis_index("col")
    return lax.div(col, 4), lax.div(row, 2), lax.rem(row, 2), lax.rem(col, 4)


def place(x, y, c, z):
    return (2 * y + c, 4 * x + z)


def block_kernel(
    mid_ref,
    grad_ref,
    block_ref,
    qkv_ref,
    routes_ref,
    w_in_ref,
    w_out_ref,
    w_qkv_ref,
    w_proj_ref,
    norm1_ref,
    norm2_ref,
    out_ref,
    w_first,
    w_second,
    mate_mid,
    mate_grad,
    mate_routes,
    outgoing,
    arrived,
    total,
    ret_in,
    choice,
    probs,
    key_t,
    window_out,
    window_in,
    context_out,
    context_in,
    heads_grad,
    final_out,
    final_in,
    l_sem,
    h_send,
    h_recv,
    m_send,
    m_recv,
    w_send,
    w_recv,
    d_send,
    d_recv,
    r_send,
    r_recv,
):
    x, y, c, z = position()
    pair = lax.div(z, 2)
    u = z + 1 - 2 * lax.rem(z, 2)
    w = 3 - z
    v = 3 - u
    other = 1 - c
    twin = place(x, y, other, z)
    me = 8 * y + 4 * pair + x
    mate = 8 * y + 4 * (1 - pair) + x

    def member(e):
        ex, ey, eb = lax.rem(e, 4), lax.div(e, 8), lax.rem(lax.div(e, 4), 2)
        differs = lax.rem(eb + pair, 2)
        return place(ex, ey, c, z + differs * (3 - 2 * z))

    row, col = lax.axis_index("row"), lax.axis_index("col")
    up, left = lax.rem(row + 7, 8), lax.rem(col + 15, 16)
    down, right = lax.rem(row + 1, 8), lax.rem(col + 1, 16)
    back = ((up, left), (up, col), (row, left))
    ahead = (None, (row, right), (down, col), (down, right))

    barrier = pltpu.get_barrier_semaphore()

    def greet(e, carry):
        @pl.when(e != me)
        def _():
            pl.semaphore_signal(barrier, inc=1, device_id=member(e), device_id_type=MESH)

        return carry

    lax.fori_loop(0, E, greet, 0)
    near = (twin, place(x, y, 0, u), place(x, y, 1, u), place(x, y, other, w))
    for where in near + back + ahead[1:]:
        pl.semaphore_signal(barrier, inc=1, device_id=where, device_id_type=MESH)
    pl.semaphore_wait(barrier, E - 1 + 10)

    def source(which, h):
        if which == 0:
            return w_in_ref.at[:, pl.ds(h * HID, HID)]
        return w_out_ref.at[pl.ds(h * HID, HID), :]

    store = (w_first, w_second)

    def ship(which, src, piece, send_at, where):
        return pltpu.make_async_remote_copy(
            src_ref=src,
            dst_ref=store[which].at[piece],
            send_sem=w_send.at[which, send_at],
            recv_sem=w_recv.at[which, piece],
            device_id=where,
            device_id_type=MESH,
        )

    def local(which, h):
        piece = 2 * z + h
        return pltpu.make_async_copy(
            source(which, h), store[which].at[piece], w_recv.at[which, piece]
        )

    inside = c == pair
    outside = jnp.logical_not(inside)

    tile = (
        (mid_ref, mate_mid),
        (grad_ref, mate_grad),
        (routes_ref, mate_routes),
    )

    def ship_tile(n):
        return pltpu.make_async_remote_copy(
            src_ref=tile[n][0],
            dst_ref=tile[n][1],
            send_sem=m_send.at[n],
            recv_sem=m_recv.at[n],
            device_id=place(x, y, c, w),
            device_id_type=MESH,
        )

    def cross(which, h):
        return ship(which, source(which, h), 2 * z + h, h, place(x, y, h, w))

    for n in range(3):
        ship_tile(n).start()

    @pl.when(outside)
    def _():
        for h in range(2):
            cross(0, h).start()

    @pl.when(inside)
    def _():
        for h in range(2):
            for which in range(2):
                ship(which, source(which, h), 2 * z + h, h, place(x, y, h, u)).start()
        for h in range(2):
            for which in range(2):
                ship(which, source(which, h), 2 * z + h, 2 + h, twin).start()
                local(which, h).start()

    def landed(which, piece):
        pltpu.make_async_copy(
            store[which].at[piece], store[which].at[piece], w_recv.at[which, piece]
        ).wait()

    def pass_on(which, piece, send_at, targets):
        landed(which, piece)
        for n, where in enumerate(targets):
            ship(which, store[which].at[piece], piece, send_at + n, where).start()

    norm2 = norm2_ref[...]

    def prepare(mid_rows, grad_rows, routes):
        grad = to_quadrants(grad_rows.astype(F32))
        mid_hat, mid_inverse = layer_stats(to_quadrants(mid_rows.astype(F32)))
        normed = (mid_hat * norm2).astype(BF16)
        ids = routes[:, 2:4].astype(jnp.int32)
        sent = [(routes[:, k : k + 1] * grad).astype(BF16) for k in range(2)]
        lanes = lax.broadcasted_iota(jnp.int32, (256, E), 1)
        hots = [(ids[:, k : k + 1] == lanes).astype(F32) for k in range(2)]
        before = (
            lax.broadcasted_iota(jnp.int32, (256, 256), 0)
            > lax.broadcasted_iota(jnp.int32, (256, 256), 1)
        ).astype(BF16)
        ranks = [dot(before, h.astype(BF16)) for h in hots]
        ranks[1] = ranks[1] + jnp.sum(hots[0], 0, keepdims=True)
        slots = [
            ids[:, k : k + 1] * C
            + jnp.sum(hots[k] * ranks[k], 1, keepdims=True).astype(jnp.int32)
            for k in range(2)
        ]
        return grad, mid_hat, mid_inverse, normed, sent, slots

    def ship_rows(at, origin, ex, ey):
        return pltpu.make_async_remote_copy(
            src_ref=outgoing.at[at],
            dst_ref=arrived.at[origin],
            send_sem=d_send.at[at],
            recv_sem=d_recv.at[origin],
            device_id=place(ex, ey, c, z),
            device_id_type=MESH,
        )

    narrow = lax.broadcasted_iota(jnp.int32, (256, 128), 1)

    def dispatch(normed, sent, slots, bit, origin):
        def one(step, carry):
            ey = lax.rem(y + step, 4)
            base = (8 * ey + 4 * pair) * C
            picks = [(slots[k] == narrow + base).astype(BF16) for k in range(2)]
            rows_n = dot(picks[0] + picks[1], normed, (0, 0))
            rows_g = dot(picks[0], sent[0], (0, 0)) + dot(picks[1], sent[1], (0, 0))
            begin = 8 * ey + 4 * bit
            outgoing[pl.ds(begin, 4), 0] = rows_n.astype(BF16).reshape(4, C, 1024)
            outgoing[pl.ds(begin, 4), 1] = rows_g.astype(BF16).reshape(4, C, 1024)

            def send_one(k, carry):
                ex = lax.rem(x + k, 4)
                at = begin + ex
                here = at == 8 * y + 4 * bit + x

                @pl.when(jnp.logical_not(here))
                def _():
                    ship_rows(at, origin, ex, ey).start()

                @pl.when(here)
                def _():
                    pltpu.make_async_copy(
                        outgoing.at[at], arrived.at[origin], d_recv.at[origin]
                    ).start()

                return carry

            return lax.fori_loop(0, 4, send_one, carry)

        lax.fori_loop(0, 4, one, 0)

    grad, mid_hat, mid_inverse, normed, sent, slots = prepare(
        mid_ref[...], grad_ref[...], routes_ref[...]
    )
    wide = lax.broadcasted_iota(jnp.int32, (256, E * C), 1)
    choice[...] = ((slots[0] == wide) | (slots[1] == wide)).astype(BF16)
    dispatch(normed, sent, slots, pair, me)
    total[...] = jnp.zeros_like(total)

    def ship_quadrant(stage, src, dst, q, where):
        return pltpu.make_async_remote_copy(
            src_ref=src.at[q],
            dst_ref=dst.at[3 - q],
            send_sem=h_send.at[stage, q],
            recv_sem=h_recv.at[stage, 3 - q],
            device_id=where,
            device_id_type=MESH,
        )

    def quadrant_landed(stage, dst, q):
        pltpu.make_async_copy(dst.at[q], dst.at[q], h_recv.at[stage, q]).wait()

    for part in range(3):
        rows = to_quadrants(qkv_ref[:, part].reshape(256, 1024).astype(F32)).astype(BF16)
        window_out[:, part] = rows.reshape(4, 64, 1024)
        window_in[0, part] = rows[192:]
    for q in range(3):
        ship_quadrant(0, window_out, window_in, q, back[q]).start()
    @pl.when(outside)
    def _():
        for h in range(2):
            cross(1, h).start()

    for q in range(1, 4):
        quadrant_landed(0, window_in, q)

    last_row = (row == 7).astype(jnp.int32)
    last_col = (col == 15).astype(jnp.int32)

    def labels(shape, dim):
        quadrant = lax.div(lax.broadcasted_iota(jnp.int32, shape, dim), 64)
        return lax.div(quadrant, 2) * (2 * last_row) + lax.rem(quadrant, 2) * last_col

    allowed = labels((256, 256), 0) == labels((256, 256), 1)
    shut = jnp.where(allowed, 0.0, -1e30)
    scale = 32**-0.5
    head_of = lax.div(lax.broadcasted_iota(jnp.int32, (256, 128), 1), 32)
    head_of_t = lax.div(lax.broadcasted_iota(jnp.int32, (128, 256), 0), 32)

    def of_head(h, rows):
        return jnp.where(head_of == h, rows, jnp.zeros_like(rows))

    def stacked(rows):
        return jnp.concatenate([of_head(h, rows) for h in range(4)], 0)

    def window_part(part, lanes_at):
        return window_in[:, part, :, lanes_at].reshape(256, 128)

    def softmax_group(group, carry):
        lanes_at = pl.ds(pl.multiple_of(group * 128, 128), 128)
        query, key = window_part(0, lanes_at), window_part(1, lanes_at)
        key_t[group] = jnp.transpose(key.astype(F32)).astype(BF16)
        products = dot(stacked(key), query, (1, 1))
        for h in range(4):
            scores = products[256 * h : 256 * h + 256] * scale + shut
            expo = jnp.exp(scores - jnp.max(scores, 0, keepdims=True))
            prob = expo * (1.0 / jnp.sum(expo, 0, keepdims=True))
            probs[group, :, 256 * h : 256 * h + 256] = prob.astype(BF16)
        return carry

    lax.fori_loop(0, HEADS // 4, softmax_group, 0)

    onward = (place(x, y, c, u), twin)
    pass_on(0, 2 * w + c, 4, onward)
    for n in range(3):
        pltpu.make_async_copy(tile[n][1], tile[n][1], m_recv.at[n]).wait()
    _, _, _, normed_m, sent_m, slots_m = prepare(
        mate_mid[...], mate_grad[...], mate_routes[...]
    )
    dispatch(normed_m, sent_m, slots_m, 1 - pair, mate)

    def product(piece, rows, begin):
        count = rows // C
        at = pl.ds(begin, count)
        normed_rows = arrived[at, 0].reshape(rows, 1024)
        grad_rows = arrived[at, 1].reshape(rows, 1024)
        first, second = w_first[piece], w_second[piece]
        pre = dot(normed_rows, first)
        act_grad = dot(grad_rows, second, (1, 1))
        pre_grad = (act_grad * gelu_slope(pre)).astype(BF16)
        return dot(pre_grad, first, (1, 1))

    def whole(piece, rows=512):
        def one(step, carry):
            at = pl.ds(pl.multiple_of(step * rows, rows), rows)
            total[at] = total[at] + product(piece, rows, step * (rows // C))
            return carry

        lax.fori_loop(0, 1024 // rows, one, 0)

    for which in range(2):
        pass_on(which, 2 * u + c, 6, (twin,))

    def rows_landed(m, carry):
        pltpu.make_async_copy(arrived.at[m], arrived.at[m], d_recv.at[m]).wait()
        return carry

    lax.fori_loop(0, E, rows_landed, 0)
    for which in range(2):
        landed(which, 2 * z)
    whole(2 * z)
    pass_on(1, 2 * w + c, 4, onward)
    for which in range(2):
        landed(which, 2 * z + 1)
    whole(2 * z + 1)
    whole(2 * u + c)
    whole(2 * w + c)
    pass_on(0, 2 * v + c, 7, (twin,))
    for which in range(2):
        landed(which, 2 * u + other)
    whole(2 * u + other)
    for which in range(2):
        landed(which, 2 * w + other)
    whole(2 * w + other)
    pass_on(1, 2 * v + c, 7, (twin,))
    whole(2 * v + c)
    for which in range(2):
        landed(which, 2 * v + other)

    def rows_gone(at, carry):
        @pl.when((at != me) & (at != mate))
        def _():
            ship_rows(at, me, x, y).wait_send()

        return carry

    lax.fori_loop(0, E, rows_gone, 0)

    def ship_back(m):
        return pltpu.make_async_remote_copy(
            src_ref=outgoing.at[m, 0],
            dst_ref=ret_in.at[me],
            send_sem=r_send.at[m],
            recv_sem=r_recv.at[me],
            device_id=member(m),
            device_id_type=MESH,
        )

    def last(step, carry):
        block = lax.rem(y + step, 4)
        at = pl.ds(pl.multiple_of(block * 256, 256), 256)
        done = total[at] + product(2 * v + other, 256, block * 8)
        outgoing[pl.ds(block * 8, 8), 0] = done.astype(BF16).reshape(8, C, 1024)

        def send_one(k, carry):
            m = block * 8 + lax.rem(4 * pair + x + k, 8)

            @pl.when(m != me)
            def _():
                ship_back(m).start()

            @pl.when(m == me)
            def _():
                pltpu.make_async_copy(
                    outgoing.at[me, 0], ret_in.at[me], r_recv.at[me]
                ).start()

            return carry

        return lax.fori_loop(0, 8, send_one, carry)

    lax.fori_loop(0, 4, last, 0)

    def gone(which, send_at):
        ship(which, store[which].at[0], 0, send_at, twin).wait_send()

    for which in range(2):
        for send_at in (0, 1, 4, 5, 6, 7):
            gone(which, send_at)

    for n in range(3):
        ship_tile(n).wait_send()

    @pl.when(inside)
    def _():
        for which in range(2):
            for send_at in (2, 3):
                gone(which, send_at)

    loads = [
        pltpu.make_async_copy(
            w_proj_ref.at[pl.ds(k * HID, HID), :], w_second.at[k], l_sem.at[k]
        )
        for k in range(2)
    ] + [
        pltpu.make_async_copy(
            w_qkv_ref.at[:, pl.ds(k * HID, HID)], w_first.at[k], l_sem.at[2 + k]
        )
        for k in range(6)
    ]
    for load in loads:
        load.start()

    def back_landed(m, carry):
        pltpu.make_async_copy(ret_in.at[m], ret_in.at[m], r_recv.at[m]).wait()
        return carry

    normed_grad = jnp.zeros((256, 1024), F32)
    for step in range(4):
        block = lax.rem(y + 4 - step, 4)
        lax.fori_loop(block * 8, block * 8 + 8, back_landed, 0)
        picked = choice[:, pl.ds(pl.multiple_of(block * 256, 256), 256)]
        rows = ret_in[pl.ds(block * 8, 8)].reshape(256, 1024)
        normed_grad = normed_grad + dot(picked, rows)
    mid_grad = grad + norm_back(normed_grad, mid_hat, mid_inverse, norm2)
    mid_grad = mid_grad.astype(BF16)

    for load in loads:
        load.wait()
    context_grad = jnp.concatenate(
        [dot(mid_grad, w_second[k], (1, 1)).astype(BF16) for k in range(2)], 1
    )
    context_out[...] = context_grad.reshape(4, 64, 1024)
    for q in range(3):
        ship_quadrant(1, context_out, context_in, q, back[q]).start()
    context_in[0] = context_grad[192:]
    in_hat, in_inverse = layer_stats(to_quadrants(block_ref[...].astype(F32)))
    for q in range(1, 4):
        quadrant_landed(1, context_in, q)

    def heads_back(group, carry):
        begin = pl.multiple_of(group * 128, 128)
        lanes_at = pl.ds(begin, 128)
        query, _, value = (window_part(part, lanes_at) for part in range(3))
        out_grad = context_in[:, :, lanes_at].reshape(256, 128)
        products = dot(stacked(value), out_grad, (1, 1))
        score_grads = []
        for h in range(4):
            prob = probs[group, :, 256 * h : 256 * h + 256].astype(F32)
            prob_grad = products[256 * h : 256 * h + 256]
            row_total = jnp.sum(prob * prob_grad, 0, keepdims=True)
            score_grads.append((prob * (prob_grad - row_total)).astype(BF16))
        turned = key_t[group]
        turned = jnp.concatenate(
            [jnp.where(head_of_t == h, turned, jnp.zeros_like(turned)) for h in range(4)], 1
        )
        sums = (
            jnp.transpose(dot(turned, jnp.concatenate(score_grads, 0))),
            dot(jnp.concatenate(score_grads, 1), stacked(query)),
            dot(probs[group], stacked(out_grad)),
        )
        for part, factor in enumerate((scale, scale, 1.0)):
            at = pl.ds(pl.multiple_of(part * 1024 + begin, 128), 128)
            heads_grad[:, at] = (sums[part] * factor).astype(BF16)
        return carry

    lax.fori_loop(0, HEADS // 4, heads_back, 0)

    def project(step, carry):
        at = pl.ds(pl.multiple_of(step * 256, 256), 256)
        part = sum(
            dot(heads_grad[:, k * HID : (k + 1) * HID], w_first[k, at, :], (1, 1))
            for k in range(6)
        )
        final_out[:, :, at] = part.astype(BF16).reshape(4, 64, 256)
        return carry

    lax.fori_loop(0, 4, project, 0)
    for q in range(1, 4):
        ship_quadrant(2, final_out, final_in, q, ahead[q]).start()
    final_in[3] = final_out[0]
    for q in range(3):
        quadrant_landed(2, final_in, q)
    upstream = final_in[...].reshape(256, 1024).astype(F32)
    result = mid_grad.astype(F32) + norm_back(upstream, in_hat, in_inverse, norm1_ref[...])
    out_ref[...] = from_quadrants(result).astype(BF16)

    def sent_all(e, carry):
        @pl.when(e != me)
        def _():
            ship_back(e).wait_send()

        return carry

    lax.fori_loop(0, E, sent_all, 0)
    for q in range(3):
        ship_quadrant(0, window_out, window_in, q, back[q]).wait_send()
        ship_quadrant(1, context_out, context_in, q, back[q]).wait_send()
        ship_quadrant(2, final_out, final_in, q + 1, ahead[q + 1]).wait_send()


def block(mid, grad, block_in, qkv, routes, w_in, w_out, w_qkv, w_proj, norm1, norm2):
    vmem = pl.BlockSpec(memory_space=pltpu.VMEM)
    anywhere = pl.BlockSpec(memory_space=pl.ANY)
    dma = pltpu.SemaphoreType.DMA
    return pl.pallas_call(
        block_kernel,
        out_shape=jax.ShapeDtypeStruct((256, 1024), BF16),
        in_specs=[vmem] * 5 + [anywhere] * 4 + [vmem] * 2,
        out_specs=vmem,
        scratch_shapes=[
            pltpu.VMEM((PIECES, 1024, HID), BF16),
            pltpu.VMEM((PIECES, HID, 1024), BF16),
            pltpu.VMEM((256, 1024), BF16),
            pltpu.VMEM((256, 1024), BF16),
            pltpu.VMEM((256, 128), F32),
            pltpu.VMEM((E, 2, C, 1024), BF16),
            pltpu.VMEM((E, 2, C, 1024), BF16),
            pltpu.VMEM((E * C, 1024), F32),
            pltpu.VMEM((E, C, 1024), BF16),
            pltpu.VMEM((256, E * C), BF16),
            pltpu.VMEM((HEADS // 4, 256, 1024), BF16),
            pltpu.VMEM((HEADS // 4, 128, 256), BF16),
            pltpu.VMEM((4, 3, 64, 1024), BF16),
            pltpu.VMEM((4, 3, 64, 1024), BF16),
            pltpu.VMEM((4, 64, 1024), BF16),
            pltpu.VMEM((4, 64, 1024), BF16),
            pltpu.VMEM((256, 3072), BF16),
            pltpu.VMEM((4, 64, 1024), BF16),
            pltpu.VMEM((4, 64, 1024), BF16),
            dma((8,)),
            dma((3, 4)),
            dma((3, 4)),
            dma((3,)),
            dma((3,)),
            dma((2, 8)),
            dma((2, 8)),
            dma((E,)),
            dma((E,)),
            dma((E,)),
            dma((E,)),
        ],
        compiler_params=pltpu.CompilerParams(
            collective_id=0, has_side_effects=True, vmem_limit_bytes=62 * 1024 * 1024
        ),
        name="block",
    )(mid, grad, block_in, qkv, routes, w_in, w_out, w_qkv, w_proj, norm1, norm2)


def shards(
    grad_out, block_in, mid, qkv, gates, expert_ids, w_in, w_out, w_qkv, w_proj, norm1, norm2
):
    window = grad_out.shape[2]
    width = grad_out.shape[4]
    count = window * window
    half = window // 2

    routes = jnp.concatenate((gates, expert_ids.astype(F32)), -1)
    routes = routes.reshape(2, half, 2, half, 4).transpose(0, 2, 1, 3, 4).reshape(count, 4)
    routes = jnp.pad(routes, ((0, 0), (0, 124)))
    result = block(
        mid.reshape(count, width),
        grad_out.reshape(count, width),
        block_in.reshape(count, width),
        qkv.reshape(window, window, 3, width).transpose(0, 2, 1, 3),
        routes,
        w_in[0],
        w_out[0],
        w_qkv,
        w_proj,
        norm1.reshape(1, width),
        norm2.reshape(1, width),
    )
    return result.reshape(grad_out.shape)


def solution(mesh):
    return jax.shard_map(
        shards,
        mesh=mesh,
        in_specs=(
            P("row", "col", None, None, None),
            P("row", "col", None, None, None),
            P("row", "col", None, None, None),
            P("row", "col", None, None, None, None),
            P("row", "col", None, None, None),
            P("row", "col", None, None, None),
            P(("row", "col"), None, None),
            P(("row", "col"), None, None),
            P(),
            P(),
            P(),
            P(),
        ),
        out_specs=P("row", "col", None, None, None),
        check_vma=False,
    )
```

```python
import jax
import jax.numpy as jnp
from jax import lax
from jax.experimental import pallas as pl
from jax.experimental.pallas import tpu as pltpu
from jax.sharding import PartitionSpec as P

HEADS = 32
E = 32
C = 32
EPSILON = 1e-05
MESH = pl.DeviceIdType.MESH
F32 = jnp.float32
BF16 = jnp.bfloat16
HID = 512
PIECES = 8


def layer_stats(values):
    floats = values.astype(F32)
    centred = floats - jnp.mean(floats, -1, keepdims=True)
    inverse = lax.rsqrt(jnp.mean(centred * centred, -1, keepdims=True) + EPSILON)
    return (centred * inverse, inverse)


def norm_back(upstream, normal_hat, inverse, gain):
    scaled_up = upstream * gain
    first = jnp.mean(scaled_up, -1, keepdims=True)
    second = jnp.mean(scaled_up * normal_hat, -1, keepdims=True)
    return inverse * (scaled_up - first - normal_hat * second)


def gelu_slope(values):
    return (
        0.5 * (1.0 + lax.erf(values * 0.7071067811865476))
        + values * jnp.exp(-0.5 * values * values) * 0.3989422804014327
    )


def dot(a, b, contract=(1, 0)):
    return lax.dot_general(
        a, b, (((contract[0],), (contract[1],)), ((), ())), preferred_element_type=F32
    )


def to_quadrants(x):
    n = x.shape[-1]
    parts = x.reshape(2, 8, 2, 8, n)
    return jnp.concatenate(
        [parts[a, :, b].reshape(64, n) for a in range(2) for b in range(2)], 0
    )


def from_quadrants(x):
    n = x.shape[-1]
    parts = x.reshape(2, 2, 8, 8, n)
    rows = []
    for a in range(2):
        for i in range(8):
            rows.append(jnp.concatenate([parts[a, 0, i], parts[a, 1, i]], 0))
    return jnp.concatenate(rows, 0)


def position():
    row, col = lax.axis_index("row"), lax.axis_index("col")
    return lax.div(col, 4), lax.div(row, 2), lax.rem(row, 2), lax.rem(col, 4)


def place(x, y, c, z):
    return (2 * y + c, 4 * x + z)


def block_kernel(
    mid_ref,
    grad_ref,
    block_ref,
    qkv_ref,
    routes_ref,
    w_in_ref,
    w_out_ref,
    w_qkv_ref,
    w_proj_ref,
    norm1_ref,
    norm2_ref,
    out_ref,
    w_first,
    w_second,
    mate_mid,
    mate_grad,
    mate_routes,
    outgoing,
    arrived,
    total,
    ret_in,
    choice,
    probs,
    key_t,
    window_out,
    window_in,
    context_out,
    context_in,
    heads_grad,
    final_out,
    final_in,
    l_sem,
    h_send,
    h_recv,
    m_send,
    m_recv,
    w_send,
    w_recv,
    d_send,
    d_recv,
    r_send,
    r_recv,
):
    x, y, c, z = position()
    pair = lax.div(z, 2)
    u = z + 1 - 2 * lax.rem(z, 2)
    w = 3 - z
    v = 3 - u
    other = 1 - c
    twin = place(x, y, other, z)
    me = 8 * y + 4 * pair + x
    mate = 8 * y + 4 * (1 - pair) + x

    def member(e):
        ex, ey, eb = lax.rem(e, 4), lax.div(e, 8), lax.rem(lax.div(e, 4), 2)
        differs = lax.rem(eb + pair, 2)
        return place(ex, ey, c, z + differs * (3 - 2 * z))

    row, col = lax.axis_index("row"), lax.axis_index("col")
    up, left = lax.rem(row + 7, 8), lax.rem(col + 15, 16)
    down, right = lax.rem(row + 1, 8), lax.rem(col + 1, 16)
    back = ((up, left), (up, col), (row, left))
    ahead = (None, (row, right), (down, col), (down, right))

    barrier = pltpu.get_barrier_semaphore()

    def greet(e, carry):
        @pl.when(e != me)
        def _():
            pl.semaphore_signal(barrier, inc=1, device_id=member(e), device_id_type=MESH)

        return carry

    lax.fori_loop(0, E, greet, 0)
    near = (twin, place(x, y, 0, u), place(x, y, 1, u), place(x, y, other, w))
    for where in near + back + ahead[1:]:
        pl.semaphore_signal(barrier, inc=1, device_id=where, device_id_type=MESH)
    pl.semaphore_wait(barrier, E - 1 + 10)

    def source(which, h):
        if which == 0:
            return w_in_ref.at[:, pl.ds(h * HID, HID)]
        return w_out_ref.at[pl.ds(h * HID, HID), :]

    store = (w_first, w_second)

    def ship(which, src, piece, send_at, where):
        return pltpu.make_async_remote_copy(
            src_ref=src,
            dst_ref=store[which].at[piece],
            send_sem=w_send.at[which, send_at],
            recv_sem=w_recv.at[which, piece],
            device_id=where,
            device_id_type=MESH,
        )

    def local(which, h):
        piece = 2 * z + h
        return pltpu.make_async_copy(
            source(which, h), store[which].at[piece], w_recv.at[which, piece]
        )

    inside = c == pair
    outside = jnp.logical_not(inside)

    tile = (
        (mid_ref, mate_mid),
        (grad_ref, mate_grad),
        (routes_ref, mate_routes),
    )

    def ship_tile(n):
        return pltpu.make_async_remote_copy(
            src_ref=tile[n][0],
            dst_ref=tile[n][1],
            send_sem=m_send.at[n],
            recv_sem=m_recv.at[n],
            device_id=place(x, y, c, w),
            device_id_type=MESH,
        )

    def cross(which, h):
        return ship(which, source(which, h), 2 * z + h, h, place(x, y, h, w))

    for n in range(3):
        ship_tile(n).start()

    @pl.when(outside)
    def _():
        for h in range(2):
            cross(0, h).start()

    @pl.when(inside)
    def _():
        for h in range(2):
            for which in range(2):
                ship(which, source(which, h), 2 * z + h, h, place(x, y, h, u)).start()
        for h in range(2):
            for which in range(2):
                ship(which, source(which, h), 2 * z + h, 2 + h, twin).start()
                local(which, h).start()

    def landed(which, piece):
        pltpu.make_async_copy(
            store[which].at[piece], store[which].at[piece], w_recv.at[which, piece]
        ).wait()

    def pass_on(which, piece, send_at, targets):
        landed(which, piece)
        for n, where in enumerate(targets):
            ship(which, store[which].at[piece], piece, send_at + n, where).start()

    norm2 = norm2_ref[...]

    def prepare(mid_rows, grad_rows, routes):
        grad = to_quadrants(grad_rows.astype(F32))
        mid_hat, mid_inverse = layer_stats(to_quadrants(mid_rows.astype(F32)))
        normed = (mid_hat * norm2).astype(BF16)
        ids = routes[:, 2:4].astype(jnp.int32)
        sent = [(routes[:, k : k + 1] * grad).astype(BF16) for k in range(2)]
        lanes = lax.broadcasted_iota(jnp.int32, (256, E), 1)
        hots = [(ids[:, k : k + 1] == lanes).astype(F32) for k in range(2)]
        before = (
            lax.broadcasted_iota(jnp.int32, (256, 256), 0)
            > lax.broadcasted_iota(jnp.int32, (256, 256), 1)
        ).astype(BF16)
        ranks = [dot(before, h.astype(BF16)) for h in hots]
        ranks[1] = ranks[1] + jnp.sum(hots[0], 0, keepdims=True)
        slots = [
            ids[:, k : k + 1] * C
            + jnp.sum(hots[k] * ranks[k], 1, keepdims=True).astype(jnp.int32)
            for k in range(2)
        ]
        return grad, mid_hat, mid_inverse, normed, sent, slots

    def ship_rows(at, origin, ex, ey):
        return pltpu.make_async_remote_copy(
            src_ref=outgoing.at[at],
            dst_ref=arrived.at[origin],
            send_sem=d_send.at[at],
            recv_sem=d_recv.at[origin],
            device_id=place(ex, ey, c, z),
            device_id_type=MESH,
        )

    narrow = lax.broadcasted_iota(jnp.int32, (256, 128), 1)

    def dispatch(normed, sent, slots, bit, origin):
        def one(step, carry):
            ey = lax.rem(y + step, 4)
            base = (8 * ey + 4 * pair) * C
            picks = [(slots[k] == narrow + base).astype(BF16) for k in range(2)]
            rows_n = dot(picks[0] + picks[1], normed, (0, 0))
            rows_g = dot(picks[0], sent[0], (0, 0)) + dot(picks[1], sent[1], (0, 0))
            begin = 8 * ey + 4 * bit
            outgoing[pl.ds(begin, 4), 0] = rows_n.astype(BF16).reshape(4, C, 1024)
            outgoing[pl.ds(begin, 4), 1] = rows_g.astype(BF16).reshape(4, C, 1024)

            def send_one(k, carry):
                ex = lax.rem(x + k, 4)
                at = begin + ex
                here = at == 8 * y + 4 * bit + x

                @pl.when(jnp.logical_not(here))
                def _():
                    ship_rows(at, origin, ex, ey).start()

                @pl.when(here)
                def _():
                    pltpu.make_async_copy(
                        outgoing.at[at], arrived.at[origin], d_recv.at[origin]
                    ).start()

                return carry

            return lax.fori_loop(0, 4, send_one, carry)

        lax.fori_loop(0, 4, one, 0)

    grad, mid_hat, mid_inverse, normed, sent, slots = prepare(
        mid_ref[...], grad_ref[...], routes_ref[...]
    )
    wide = lax.broadcasted_iota(jnp.int32, (256, E * C), 1)
    choice[...] = ((slots[0] == wide) | (slots[1] == wide)).astype(BF16)
    dispatch(normed, sent, slots, pair, me)
    total[...] = jnp.zeros_like(total)

    def ship_quadrant(stage, src, dst, q, where):
        return pltpu.make_async_remote_copy(
            src_ref=src.at[q],
            dst_ref=dst.at[3 - q],
            send_sem=h_send.at[stage, q],
            recv_sem=h_recv.at[stage, 3 - q],
            device_id=where,
            device_id_type=MESH,
        )

    def quadrant_landed(stage, dst, q):
        pltpu.make_async_copy(dst.at[q], dst.at[q], h_recv.at[stage, q]).wait()

    for part in range(3):
        rows = to_quadrants(qkv_ref[:, part].reshape(256, 1024).astype(F32)).astype(BF16)
        window_out[:, part] = rows.reshape(4, 64, 1024)
        window_in[0, part] = rows[192:]
    for q in range(3):
        ship_quadrant(0, window_out, window_in, q, back[q]).start()
    for q in range(1, 4):
        quadrant_landed(0, window_in, q)

    last_row = (row == 7).astype(jnp.int32)
    last_col = (col == 15).astype(jnp.int32)

    def labels(shape, dim):
        quadrant = lax.div(lax.broadcasted_iota(jnp.int32, shape, dim), 64)
        return lax.div(quadrant, 2) * (2 * last_row) + lax.rem(quadrant, 2) * last_col

    allowed = labels((256, 256), 0) == labels((256, 256), 1)
    shut = jnp.where(allowed, 0.0, -1e30)
    scale = 32**-0.5
    head_of = lax.div(lax.broadcasted_iota(jnp.int32, (256, 128), 1), 32)
    head_of_t = lax.div(lax.broadcasted_iota(jnp.int32, (128, 256), 0), 32)

    def of_head(h, rows):
        return jnp.where(head_of == h, rows, jnp.zeros_like(rows))

    def stacked(rows):
        return jnp.concatenate([of_head(h, rows) for h in range(4)], 0)

    def window_part(part, lanes_at):
        return window_in[:, part, :, lanes_at].reshape(256, 128)

    def softmax_group(group, carry):
        lanes_at = pl.ds(pl.multiple_of(group * 128, 128), 128)
        query, key = window_part(0, lanes_at), window_part(1, lanes_at)
        key_t[group] = jnp.transpose(key.astype(F32)).astype(BF16)
        products = dot(stacked(key), query, (1, 1))
        for h in range(4):
            scores = products[256 * h : 256 * h + 256] * scale + shut
            expo = jnp.exp(scores - jnp.max(scores, 0, keepdims=True))
            prob = expo * (1.0 / jnp.sum(expo, 0, keepdims=True))
            probs[group, :, 256 * h : 256 * h + 256] = prob.astype(BF16)
        return carry

    lax.fori_loop(0, HEADS // 4, softmax_group, 0)

    @pl.when(outside)
    def _():
        for h in range(2):
            cross(1, h).start()

    onward = (place(x, y, c, u), twin)
    pass_on(0, 2 * w + c, 4, onward)
    for n in range(3):
        pltpu.make_async_copy(tile[n][1], tile[n][1], m_recv.at[n]).wait()
    _, _, _, normed_m, sent_m, slots_m = prepare(
        mate_mid[...], mate_grad[...], mate_routes[...]
    )
    dispatch(normed_m, sent_m, slots_m, 1 - pair, mate)

    def product(piece, rows, begin):
        count = rows // C
        at = pl.ds(begin, count)
        normed_rows = arrived[at, 0].reshape(rows, 1024)
        grad_rows = arrived[at, 1].reshape(rows, 1024)
        first, second = w_first[piece], w_second[piece]
        pre = dot(normed_rows, first)
        act_grad = dot(grad_rows, second, (1, 1))
        pre_grad = (act_grad * gelu_slope(pre)).astype(BF16)
        return dot(pre_grad, first, (1, 1))

    def whole(piece, rows=512):
        def one(step, carry):
            at = pl.ds(pl.multiple_of(step * rows, rows), rows)
            total[at] = total[at] + product(piece, rows, step * (rows // C))
            return carry

        lax.fori_loop(0, 1024 // rows, one, 0)

    for which in range(2):
        pass_on(which, 2 * u + c, 6, (twin,))
    pass_on(1, 2 * w + c, 4, onward)

    def rows_landed(m, carry):
        pltpu.make_async_copy(arrived.at[m], arrived.at[m], d_recv.at[m]).wait()
        return carry

    lax.fori_loop(0, E, rows_landed, 0)
    for which in range(2):
        landed(which, 2 * z)
    whole(2 * z)
    for which in range(2):
        landed(which, 2 * z + 1)
    whole(2 * z + 1)
    whole(2 * u + c)
    whole(2 * w + c)
    pass_on(0, 2 * v + c, 7, (twin,))
    for which in range(2):
        landed(which, 2 * u + other)
    whole(2 * u + other)
    for which in range(2):
        landed(which, 2 * w + other)
    whole(2 * w + other)
    pass_on(1, 2 * v + c, 7, (twin,))
    whole(2 * v + c)
    for which in range(2):
        landed(which, 2 * v + other)

    def rows_gone(at, carry):
        @pl.when((at != me) & (at != mate))
        def _():
            ship_rows(at, me, x, y).wait_send()

        return carry

    lax.fori_loop(0, E, rows_gone, 0)

    def ship_back(m):
        return pltpu.make_async_remote_copy(
            src_ref=outgoing.at[m, 0],
            dst_ref=ret_in.at[me],
            send_sem=r_send.at[m],
            recv_sem=r_recv.at[me],
            device_id=member(m),
            device_id_type=MESH,
        )

    def last(step, carry):
        block = lax.rem(y + step, 4)
        at = pl.ds(pl.multiple_of(block * 256, 256), 256)
        done = total[at] + product(2 * v + other, 256, block * 8)
        outgoing[pl.ds(block * 8, 8), 0] = done.astype(BF16).reshape(8, C, 1024)

        def send_one(k, carry):
            m = block * 8 + lax.rem(4 * pair + x + k, 8)

            @pl.when(m != me)
            def _():
                ship_back(m).start()

            @pl.when(m == me)
            def _():
                pltpu.make_async_copy(
                    outgoing.at[me, 0], ret_in.at[me], r_recv.at[me]
                ).start()

            return carry

        return lax.fori_loop(0, 8, send_one, carry)

    lax.fori_loop(0, 4, last, 0)

    def gone(which, send_at):
        ship(which, store[which].at[0], 0, send_at, twin).wait_send()

    for which in range(2):
        for send_at in (0, 1, 4, 5, 6, 7):
            gone(which, send_at)

    for n in range(3):
        ship_tile(n).wait_send()

    @pl.when(inside)
    def _():
        for which in range(2):
            for send_at in (2, 3):
                gone(which, send_at)

    loads = [
        pltpu.make_async_copy(
            w_proj_ref.at[pl.ds(k * HID, HID), :], w_second.at[k], l_sem.at[k]
        )
        for k in range(2)
    ] + [
        pltpu.make_async_copy(
            w_qkv_ref.at[:, pl.ds(k * HID, HID)], w_first.at[k], l_sem.at[2 + k]
        )
        for k in range(6)
    ]
    for load in loads:
        load.start()

    def back_landed(m, carry):
        pltpu.make_async_copy(ret_in.at[m], ret_in.at[m], r_recv.at[m]).wait()
        return carry

    normed_grad = jnp.zeros((256, 1024), F32)
    for step in range(4):
        block = lax.rem(y + 4 - step, 4)
        lax.fori_loop(block * 8, block * 8 + 8, back_landed, 0)
        picked = choice[:, pl.ds(pl.multiple_of(block * 256, 256), 256)]
        rows = ret_in[pl.ds(block * 8, 8)].reshape(256, 1024)
        normed_grad = normed_grad + dot(picked, rows)
    mid_grad = grad + norm_back(normed_grad, mid_hat, mid_inverse, norm2)
    mid_grad = mid_grad.astype(BF16)

    for load in loads:
        load.wait()
    context_grad = jnp.concatenate(
        [dot(mid_grad, w_second[k], (1, 1)).astype(BF16) for k in range(2)], 1
    )
    context_out[...] = context_grad.reshape(4, 64, 1024)
    for q in range(3):
        ship_quadrant(1, context_out, context_in, q, back[q]).start()
    context_in[0] = context_grad[192:]
    in_hat, in_inverse = layer_stats(to_quadrants(block_ref[...].astype(F32)))
    for q in range(1, 4):
        quadrant_landed(1, context_in, q)

    def heads_back(group, carry):
        begin = pl.multiple_of(group * 128, 128)
        lanes_at = pl.ds(begin, 128)
        query, _, value = (window_part(part, lanes_at) for part in range(3))
        out_grad = context_in[:, :, lanes_at].reshape(256, 128)
        products = dot(stacked(value), out_grad, (1, 1))
        score_grads = []
        for h in range(4):
            prob = probs[group, :, 256 * h : 256 * h + 256].astype(F32)
            prob_grad = products[256 * h : 256 * h + 256]
            row_total = jnp.sum(prob * prob_grad, 0, keepdims=True)
            score_grads.append((prob * (prob_grad - row_total)).astype(BF16))
        turned = key_t[group]
        turned = jnp.concatenate(
            [jnp.where(head_of_t == h, turned, jnp.zeros_like(turned)) for h in range(4)], 1
        )
        sums = (
            jnp.transpose(dot(turned, jnp.concatenate(score_grads, 0))),
            dot(jnp.concatenate(score_grads, 1), stacked(query)),
            dot(probs[group], stacked(out_grad)),
        )
        for part, factor in enumerate((scale, scale, 1.0)):
            at = pl.ds(pl.multiple_of(part * 1024 + begin, 128), 128)
            heads_grad[:, at] = (sums[part] * factor).astype(BF16)
        return carry

    lax.fori_loop(0, HEADS // 4, heads_back, 0)

    def project(step, carry):
        at = pl.ds(pl.multiple_of(step * 256, 256), 256)
        part = sum(
            dot(heads_grad[:, k * HID : (k + 1) * HID], w_first[k, at, :], (1, 1))
            for k in range(6)
        )
        final_out[:, :, at] = part.astype(BF16).reshape(4, 64, 256)
        return carry

    lax.fori_loop(0, 4, project, 0)
    for q in range(1, 4):
        ship_quadrant(2, final_out, final_in, q, ahead[q]).start()
    final_in[3] = final_out[0]
    for q in range(3):
        quadrant_landed(2, final_in, q)
    upstream = final_in[...].reshape(256, 1024).astype(F32)
    result = mid_grad.astype(F32) + norm_back(upstream, in_hat, in_inverse, norm1_ref[...])
    out_ref[...] = from_quadrants(result).astype(BF16)

    def sent_all(e, carry):
        @pl.when(e != me)
        def _():
            ship_back(e).wait_send()

        return carry

    lax.fori_loop(0, E, sent_all, 0)
    for q in range(3):
        ship_quadrant(0, window_out, window_in, q, back[q]).wait_send()
        ship_quadrant(1, context_out, context_in, q, back[q]).wait_send()
        ship_quadrant(2, final_out, final_in, q + 1, ahead[q + 1]).wait_send()


def block(mid, grad, block_in, qkv, routes, w_in, w_out, w_qkv, w_proj, norm1, norm2):
    vmem = pl.BlockSpec(memory_space=pltpu.VMEM)
    anywhere = pl.BlockSpec(memory_space=pl.ANY)
    dma = pltpu.SemaphoreType.DMA
    return pl.pallas_call(
        block_kernel,
        out_shape=jax.ShapeDtypeStruct((256, 1024), BF16),
        in_specs=[vmem] * 5 + [anywhere] * 4 + [vmem] * 2,
        out_specs=vmem,
        scratch_shapes=[
            pltpu.VMEM((PIECES, 1024, HID), BF16),
            pltpu.VMEM((PIECES, HID, 1024), BF16),
            pltpu.VMEM((256, 1024), BF16),
            pltpu.VMEM((256, 1024), BF16),
            pltpu.VMEM((256, 128), F32),
            pltpu.VMEM((E, 2, C, 1024), BF16),
            pltpu.VMEM((E, 2, C, 1024), BF16),
            pltpu.VMEM((E * C, 1024), F32),
            pltpu.VMEM((E, C, 1024), BF16),
            pltpu.VMEM((256, E * C), BF16),
            pltpu.VMEM((HEADS // 4, 256, 1024), BF16),
            pltpu.VMEM((HEADS // 4, 128, 256), BF16),
            pltpu.VMEM((4, 3, 64, 1024), BF16),
            pltpu.VMEM((4, 3, 64, 1024), BF16),
            pltpu.VMEM((4, 64, 1024), BF16),
            pltpu.VMEM((4, 64, 1024), BF16),
            pltpu.VMEM((256, 3072), BF16),
            pltpu.VMEM((4, 64, 1024), BF16),
            pltpu.VMEM((4, 64, 1024), BF16),
            dma((8,)),
            dma((3, 4)),
            dma((3, 4)),
            dma((3,)),
            dma((3,)),
            dma((2, 8)),
            dma((2, 8)),
            dma((E,)),
            dma((E,)),
            dma((E,)),
            dma((E,)),
        ],
        compiler_params=pltpu.CompilerParams(
            collective_id=0, has_side_effects=True, vmem_limit_bytes=62 * 1024 * 1024
        ),
        name="block",
    )(mid, grad, block_in, qkv, routes, w_in, w_out, w_qkv, w_proj, norm1, norm2)


def shards(
    grad_out, block_in, mid, qkv, gates, expert_ids, w_in, w_out, w_qkv, w_proj, norm1, norm2
):
    window = grad_out.shape[2]
    width = grad_out.shape[4]
    count = window * window
    half = window // 2

    routes = jnp.concatenate((gates, expert_ids.astype(F32)), -1)
    routes = routes.reshape(2, half, 2, half, 4).transpose(0, 2, 1, 3, 4).reshape(count, 4)
    routes = jnp.pad(routes, ((0, 0), (0, 124)))
    result = block(
        mid.reshape(count, width),
        grad_out.reshape(count, width),
        block_in.reshape(count, width),
        qkv.reshape(window, window, 3, width).transpose(0, 2, 1, 3),
        routes,
        w_in[0],
        w_out[0],
        w_qkv,
        w_proj,
        norm1.reshape(1, width),
        norm2.reshape(1, width),
    )
    return result.reshape(grad_out.shape)


def solution(mesh):
    return jax.shard_map(
        shards,
        mesh=mesh,
        in_specs=(
            P("row", "col", None, None, None),
            P("row", "col", None, None, None),
            P("row", "col", None, None, None),
            P("row", "col", None, None, None, None),
            P("row", "col", None, None, None),
            P("row", "col", None, None, None),
            P(("row", "col"), None, None),
            P(("row", "col"), None, None),
            P(),
            P(),
            P(),
            P(),
        ),
        out_specs=P("row", "col", None, None, None),
        check_vma=False,
    )
```

```python
import jax
import jax.numpy as jnp
from jax import lax
from jax.experimental import pallas as pl
from jax.experimental.pallas import tpu as pltpu
from jax.sharding import PartitionSpec as P

HEADS = 32
E = 32
C = 32
EPSILON = 1e-05
MESH = pl.DeviceIdType.MESH
F32 = jnp.float32
BF16 = jnp.bfloat16
HID = 512
PIECES = 8


def layer_stats(values):
    floats = values.astype(F32)
    centred = floats - jnp.mean(floats, -1, keepdims=True)
    inverse = lax.rsqrt(jnp.mean(centred * centred, -1, keepdims=True) + EPSILON)
    return (centred * inverse, inverse)


def norm_back(upstream, normal_hat, inverse, gain):
    scaled_up = upstream * gain
    first = jnp.mean(scaled_up, -1, keepdims=True)
    second = jnp.mean(scaled_up * normal_hat, -1, keepdims=True)
    return inverse * (scaled_up - first - normal_hat * second)


def gelu_slope(values):
    return (
        0.5 * (1.0 + lax.erf(values * 0.7071067811865476))
        + values * jnp.exp(-0.5 * values * values) * 0.3989422804014327
    )


def dot(a, b, contract=(1, 0)):
    return lax.dot_general(
        a, b, (((contract[0],), (contract[1],)), ((), ())), preferred_element_type=F32
    )


def to_quadrants(x):
    n = x.shape[-1]
    parts = x.reshape(2, 8, 2, 8, n)
    return jnp.concatenate(
        [parts[a, :, b].reshape(64, n) for a in range(2) for b in range(2)], 0
    )


def from_quadrants(x):
    n = x.shape[-1]
    parts = x.reshape(2, 2, 8, 8, n)
    rows = []
    for a in range(2):
        for i in range(8):
            rows.append(jnp.concatenate([parts[a, 0, i], parts[a, 1, i]], 0))
    return jnp.concatenate(rows, 0)


def position():
    row, col = lax.axis_index("row"), lax.axis_index("col")
    return lax.div(col, 4), lax.div(row, 2), lax.rem(row, 2), lax.rem(col, 4)


def place(x, y, c, z):
    return (2 * y + c, 4 * x + z)


def block_kernel(
    mid_ref,
    grad_ref,
    block_ref,
    qkv_ref,
    routes_ref,
    w_in_ref,
    w_out_ref,
    w_qkv_ref,
    w_proj_ref,
    norm1_ref,
    norm2_ref,
    out_ref,
    w_first,
    w_second,
    mate_mid,
    mate_grad,
    mate_routes,
    outgoing,
    arrived,
    total,
    ret_in,
    choice,
    slopes,
    probs,
    key_t,
    window_out,
    window_in,
    context_out,
    context_in,
    heads_grad,
    final_out,
    final_in,
    l_sem,
    h_send,
    h_recv,
    m_send,
    m_recv,
    w_send,
    w_recv,
    d_send,
    d_recv,
    r_send,
    r_recv,
):
    x, y, c, z = position()
    pair = lax.div(z, 2)
    u = z + 1 - 2 * lax.rem(z, 2)
    w = 3 - z
    v = 3 - u
    other = 1 - c
    twin = place(x, y, other, z)
    me = 8 * y + 4 * pair + x
    mate = 8 * y + 4 * (1 - pair) + x

    def member(e):
        ex, ey, eb = lax.rem(e, 4), lax.div(e, 8), lax.rem(lax.div(e, 4), 2)
        differs = lax.rem(eb + pair, 2)
        return place(ex, ey, c, z + differs * (3 - 2 * z))

    row, col = lax.axis_index("row"), lax.axis_index("col")
    up, left = lax.rem(row + 7, 8), lax.rem(col + 15, 16)
    down, right = lax.rem(row + 1, 8), lax.rem(col + 1, 16)
    back = ((up, left), (up, col), (row, left))
    ahead = (None, (row, right), (down, col), (down, right))

    barrier = pltpu.get_barrier_semaphore()

    def greet(e, carry):
        @pl.when(e != me)
        def _():
            pl.semaphore_signal(barrier, inc=1, device_id=member(e), device_id_type=MESH)

        return carry

    lax.fori_loop(0, E, greet, 0)
    near = (twin, place(x, y, 0, u), place(x, y, 1, u), place(x, y, other, w))
    for where in near + back + ahead[1:]:
        pl.semaphore_signal(barrier, inc=1, device_id=where, device_id_type=MESH)
    pl.semaphore_wait(barrier, E - 1 + 10)

    def source(which, h):
        if which == 0:
            return w_in_ref.at[:, pl.ds(h * HID, HID)]
        return w_out_ref.at[pl.ds(h * HID, HID), :]

    store = (w_first, w_second)

    def ship(which, src, piece, send_at, where):
        return pltpu.make_async_remote_copy(
            src_ref=src,
            dst_ref=store[which].at[piece],
            send_sem=w_send.at[which, send_at],
            recv_sem=w_recv.at[which, piece],
            device_id=where,
            device_id_type=MESH,
        )

    def local(which, h):
        piece = 2 * z + h
        return pltpu.make_async_copy(
            source(which, h), store[which].at[piece], w_recv.at[which, piece]
        )

    inside = c == pair
    outside = jnp.logical_not(inside)

    tile = (
        (mid_ref, mate_mid),
        (grad_ref, mate_grad),
        (routes_ref, mate_routes),
    )

    def ship_tile(n):
        return pltpu.make_async_remote_copy(
            src_ref=tile[n][0],
            dst_ref=tile[n][1],
            send_sem=m_send.at[n],
            recv_sem=m_recv.at[n],
            device_id=place(x, y, c, w),
            device_id_type=MESH,
        )

    def cross(which, h):
        return ship(which, source(which, h), 2 * z + h, h, place(x, y, h, w))

    for n in range(3):
        ship_tile(n).start()

    @pl.when(outside)
    def _():
        for h in range(2):
            cross(0, h).start()

    @pl.when(inside)
    def _():
        for h in range(2):
            for which in range(2):
                ship(which, source(which, h), 2 * z + h, h, place(x, y, h, u)).start()
        for h in range(2):
            for which in range(2):
                ship(which, source(which, h), 2 * z + h, 2 + h, twin).start()
                local(which, h).start()

    def landed(which, piece):
        pltpu.make_async_copy(
            store[which].at[piece], store[which].at[piece], w_recv.at[which, piece]
        ).wait()

    def pass_on(which, piece, send_at, targets):
        landed(which, piece)
        for n, where in enumerate(targets):
            ship(which, store[which].at[piece], piece, send_at + n, where).start()

    norm2 = norm2_ref[...]

    def prepare(mid_rows, grad_rows, routes):
        grad = to_quadrants(grad_rows.astype(F32))
        mid_hat, mid_inverse = layer_stats(to_quadrants(mid_rows.astype(F32)))
        normed = (mid_hat * norm2).astype(BF16)
        ids = routes[:, 2:4].astype(jnp.int32)
        sent = [(routes[:, k : k + 1] * grad).astype(BF16) for k in range(2)]
        lanes = lax.broadcasted_iota(jnp.int32, (256, E), 1)
        hots = [(ids[:, k : k + 1] == lanes).astype(F32) for k in range(2)]
        before = (
            lax.broadcasted_iota(jnp.int32, (256, 256), 0)
            > lax.broadcasted_iota(jnp.int32, (256, 256), 1)
        ).astype(BF16)
        ranks = [dot(before, h.astype(BF16)) for h in hots]
        ranks[1] = ranks[1] + jnp.sum(hots[0], 0, keepdims=True)
        slots = [
            ids[:, k : k + 1] * C
            + jnp.sum(hots[k] * ranks[k], 1, keepdims=True).astype(jnp.int32)
            for k in range(2)
        ]
        return grad, mid_hat, mid_inverse, normed, sent, slots

    def ship_rows(at, origin, ex, ey):
        return pltpu.make_async_remote_copy(
            src_ref=outgoing.at[at],
            dst_ref=arrived.at[origin],
            send_sem=d_send.at[at],
            recv_sem=d_recv.at[origin],
            device_id=place(ex, ey, c, z),
            device_id_type=MESH,
        )

    narrow = lax.broadcasted_iota(jnp.int32, (256, 128), 1)

    def dispatch(normed, sent, slots, bit, origin):
        def one(step, carry):
            ey = lax.rem(y + step, 4)
            base = (8 * ey + 4 * pair) * C
            picks = [(slots[k] == narrow + base).astype(BF16) for k in range(2)]
            rows_n = dot(picks[0] + picks[1], normed, (0, 0))
            rows_g = dot(picks[0], sent[0], (0, 0)) + dot(picks[1], sent[1], (0, 0))
            begin = 8 * ey + 4 * bit
            outgoing[pl.ds(begin, 4), 0] = rows_n.astype(BF16).reshape(4, C, 1024)
            outgoing[pl.ds(begin, 4), 1] = rows_g.astype(BF16).reshape(4, C, 1024)

            def send_one(k, carry):
                ex = lax.rem(x + k, 4)
                at = begin + ex
                here = at == 8 * y + 4 * bit + x

                @pl.when(jnp.logical_not(here))
                def _():
                    ship_rows(at, origin, ex, ey).start()

                @pl.when(here)
                def _():
                    pltpu.make_async_copy(
                        outgoing.at[at], arrived.at[origin], d_recv.at[origin]
                    ).start()

                return carry

            return lax.fori_loop(0, 4, send_one, carry)

        lax.fori_loop(0, 4, one, 0)

    grad, mid_hat, mid_inverse, normed, sent, slots = prepare(
        mid_ref[...], grad_ref[...], routes_ref[...]
    )
    wide = lax.broadcasted_iota(jnp.int32, (256, E * C), 1)
    choice[...] = ((slots[0] == wide) | (slots[1] == wide)).astype(BF16)
    dispatch(normed, sent, slots, pair, me)
    total[...] = jnp.zeros_like(total)

    def ship_quadrant(stage, src, dst, q, where):
        return pltpu.make_async_remote_copy(
            src_ref=src.at[q],
            dst_ref=dst.at[3 - q],
            send_sem=h_send.at[stage, q],
            recv_sem=h_recv.at[stage, 3 - q],
            device_id=where,
            device_id_type=MESH,
        )

    def quadrant_landed(stage, dst, q):
        pltpu.make_async_copy(dst.at[q], dst.at[q], h_recv.at[stage, q]).wait()

    for part in range(3):
        rows = to_quadrants(qkv_ref[:, part].reshape(256, 1024).astype(F32)).astype(BF16)
        window_out[:, part] = rows.reshape(4, 64, 1024)
        window_in[0, part] = rows[192:]
    for q in range(3):
        ship_quadrant(0, window_out, window_in, q, back[q]).start()
    for q in range(1, 4):
        quadrant_landed(0, window_in, q)

    last_row = (row == 7).astype(jnp.int32)
    last_col = (col == 15).astype(jnp.int32)

    def labels(shape, dim):
        quadrant = lax.div(lax.broadcasted_iota(jnp.int32, shape, dim), 64)
        return lax.div(quadrant, 2) * (2 * last_row) + lax.rem(quadrant, 2) * last_col

    allowed = labels((256, 256), 0) == labels((256, 256), 1)
    shut = jnp.where(allowed, 0.0, -1e30)
    scale = 32**-0.5
    head_of = lax.div(lax.broadcasted_iota(jnp.int32, (256, 128), 1), 32)
    head_of_t = lax.div(lax.broadcasted_iota(jnp.int32, (128, 256), 0), 32)

    def of_head(h, rows):
        return jnp.where(head_of == h, rows, jnp.zeros_like(rows))

    def stacked(rows):
        return jnp.concatenate([of_head(h, rows) for h in range(4)], 0)

    def window_part(part, lanes_at):
        return window_in[:, part, :, lanes_at].reshape(256, 128)

    def softmax_group(group, carry):
        lanes_at = pl.ds(pl.multiple_of(group * 128, 128), 128)
        query, key = window_part(0, lanes_at), window_part(1, lanes_at)
        key_t[group] = jnp.transpose(key.astype(F32)).astype(BF16)
        products = dot(stacked(key), query, (1, 1))
        for h in range(4):
            scores = products[256 * h : 256 * h + 256] * scale + shut
            expo = jnp.exp(scores - jnp.max(scores, 0, keepdims=True))
            prob = expo * (1.0 / jnp.sum(expo, 0, keepdims=True))
            probs[group, :, 256 * h : 256 * h + 256] = prob.astype(BF16)
        return carry

    lax.fori_loop(0, HEADS // 4, softmax_group, 0)

    @pl.when(outside)
    def _():
        for h in range(2):
            cross(1, h).start()

    onward = (place(x, y, c, u), twin)
    pass_on(0, 2 * w + c, 4, onward)
    for n in range(3):
        pltpu.make_async_copy(tile[n][1], tile[n][1], m_recv.at[n]).wait()
    _, _, _, normed_m, sent_m, slots_m = prepare(
        mate_mid[...], mate_grad[...], mate_routes[...]
    )
    dispatch(normed_m, sent_m, slots_m, 1 - pair, mate)

    def product(piece, rows, begin, known=None):
        count = rows // C
        at = pl.ds(begin, count)
        normed_rows = arrived[at, 0].reshape(rows, 1024)
        grad_rows = arrived[at, 1].reshape(rows, 1024)
        first, second = w_first[piece], w_second[piece]
        if known is None:
            slope = gelu_slope(dot(normed_rows, first))
        else:
            slope = slopes[known, pl.ds(pl.multiple_of(begin * C, 256), rows)]
        act_grad = dot(grad_rows, second, (1, 1))
        pre_grad = (act_grad * slope).astype(BF16)
        return dot(pre_grad, first, (1, 1))

    def slopes_of(known, piece):
        def one(step, carry):
            rows = arrived[pl.ds(step * 16, 16), 0].reshape(512, 1024)
            at = pl.ds(pl.multiple_of(step * 512, 512), 512)
            slopes[known, at] = gelu_slope(dot(rows, w_first[piece]))
            return carry

        lax.fori_loop(0, 2, one, 0)

    def whole(piece, rows=512, known=None):
        def one(step, carry):
            at = pl.ds(pl.multiple_of(step * rows, rows), rows)
            total[at] = total[at] + product(piece, rows, step * (rows // C), known)
            return carry

        lax.fori_loop(0, 1024 // rows, one, 0)

    for which in range(2):
        pass_on(which, 2 * u + c, 6, (twin,))
    pass_on(1, 2 * w + c, 4, onward)

    def rows_landed(m, carry):
        pltpu.make_async_copy(arrived.at[m], arrived.at[m], d_recv.at[m]).wait()
        return carry

    lax.fori_loop(0, E, rows_landed, 0)
    for which in range(2):
        landed(which, 2 * z)
    whole(2 * z)
    for which in range(2):
        landed(which, 2 * z + 1)
    whole(2 * z + 1)
    whole(2 * u + c)
    whole(2 * w + c)
    pass_on(0, 2 * v + c, 7, (twin,))
    for which in range(2):
        landed(which, 2 * u + other)
    whole(2 * u + other)
    for which in range(2):
        landed(which, 2 * w + other)
    whole(2 * w + other)
    slopes_of(0, 2 * v + c)
    landed(0, 2 * v + other)
    slopes_of(1, 2 * v + other)
    pass_on(1, 2 * v + c, 7, (twin,))
    whole(2 * v + c, known=0)
    landed(1, 2 * v + other)

    def rows_gone(at, carry):
        @pl.when((at != me) & (at != mate))
        def _():
            ship_rows(at, me, x, y).wait_send()

        return carry

    lax.fori_loop(0, E, rows_gone, 0)

    def ship_back(m):
        return pltpu.make_async_remote_copy(
            src_ref=outgoing.at[m, 0],
            dst_ref=ret_in.at[me],
            send_sem=r_send.at[m],
            recv_sem=r_recv.at[me],
            device_id=member(m),
            device_id_type=MESH,
        )

    def last(step, carry):
        block = lax.rem(y + step, 4)
        at = pl.ds(pl.multiple_of(block * 256, 256), 256)
        done = total[at] + product(2 * v + other, 256, block * 8, 1)
        outgoing[pl.ds(block * 8, 8), 0] = done.astype(BF16).reshape(8, C, 1024)

        def send_one(k, carry):
            m = block * 8 + lax.rem(4 * pair + x + k, 8)

            @pl.when(m != me)
            def _():
                ship_back(m).start()

            @pl.when(m == me)
            def _():
                pltpu.make_async_copy(
                    outgoing.at[me, 0], ret_in.at[me], r_recv.at[me]
                ).start()

            return carry

        return lax.fori_loop(0, 8, send_one, carry)

    lax.fori_loop(0, 4, last, 0)

    def gone(which, send_at):
        ship(which, store[which].at[0], 0, send_at, twin).wait_send()

    for which in range(2):
        for send_at in (0, 1, 4, 5, 6, 7):
            gone(which, send_at)

    for n in range(3):
        ship_tile(n).wait_send()

    @pl.when(inside)
    def _():
        for which in range(2):
            for send_at in (2, 3):
                gone(which, send_at)

    loads = [
        pltpu.make_async_copy(
            w_proj_ref.at[pl.ds(k * HID, HID), :], w_second.at[k], l_sem.at[k]
        )
        for k in range(2)
    ] + [
        pltpu.make_async_copy(
            w_qkv_ref.at[:, pl.ds(k * HID, HID)], w_first.at[k], l_sem.at[2 + k]
        )
        for k in range(6)
    ]
    for load in loads:
        load.start()

    def back_landed(m, carry):
        pltpu.make_async_copy(ret_in.at[m], ret_in.at[m], r_recv.at[m]).wait()
        return carry

    normed_grad = jnp.zeros((256, 1024), F32)
    for step in range(4):
        block = lax.rem(y + 4 - step, 4)
        lax.fori_loop(block * 8, block * 8 + 8, back_landed, 0)
        picked = choice[:, pl.ds(pl.multiple_of(block * 256, 256), 256)]
        rows = ret_in[pl.ds(block * 8, 8)].reshape(256, 1024)
        normed_grad = normed_grad + dot(picked, rows)
    mid_grad = grad + norm_back(normed_grad, mid_hat, mid_inverse, norm2)
    mid_grad = mid_grad.astype(BF16)

    for load in loads:
        load.wait()
    context_grad = jnp.concatenate(
        [dot(mid_grad, w_second[k], (1, 1)).astype(BF16) for k in range(2)], 1
    )
    context_out[...] = context_grad.reshape(4, 64, 1024)
    for q in range(3):
        ship_quadrant(1, context_out, context_in, q, back[q]).start()
    context_in[0] = context_grad[192:]
    in_hat, in_inverse = layer_stats(to_quadrants(block_ref[...].astype(F32)))
    for q in range(1, 4):
        quadrant_landed(1, context_in, q)

    def heads_back(group, carry):
        begin = pl.multiple_of(group * 128, 128)
        lanes_at = pl.ds(begin, 128)
        query, _, value = (window_part(part, lanes_at) for part in range(3))
        out_grad = context_in[:, :, lanes_at].reshape(256, 128)
        products = dot(stacked(value), out_grad, (1, 1))
        score_grads = []
        for h in range(4):
            prob = probs[group, :, 256 * h : 256 * h + 256].astype(F32)
            prob_grad = products[256 * h : 256 * h + 256]
            row_total = jnp.sum(prob * prob_grad, 0, keepdims=True)
            score_grads.append((prob * (prob_grad - row_total)).astype(BF16))
        turned = key_t[group]
        turned = jnp.concatenate(
            [jnp.where(head_of_t == h, turned, jnp.zeros_like(turned)) for h in range(4)], 1
        )
        sums = (
            jnp.transpose(dot(turned, jnp.concatenate(score_grads, 0))),
            dot(jnp.concatenate(score_grads, 1), stacked(query)),
            dot(probs[group], stacked(out_grad)),
        )
        for part, factor in enumerate((scale, scale, 1.0)):
            at = pl.ds(pl.multiple_of(part * 1024 + begin, 128), 128)
            heads_grad[:, at] = (sums[part] * factor).astype(BF16)
        return carry

    lax.fori_loop(0, HEADS // 4, heads_back, 0)

    def project(step, carry):
        at = pl.ds(pl.multiple_of(step * 256, 256), 256)
        part = sum(
            dot(heads_grad[:, k * HID : (k + 1) * HID], w_first[k, at, :], (1, 1))
            for k in range(6)
        )
        final_out[:, :, at] = part.astype(BF16).reshape(4, 64, 256)
        return carry

    lax.fori_loop(0, 4, project, 0)
    for q in range(1, 4):
        ship_quadrant(2, final_out, final_in, q, ahead[q]).start()
    final_in[3] = final_out[0]
    for q in range(3):
        quadrant_landed(2, final_in, q)
    upstream = final_in[...].reshape(256, 1024).astype(F32)
    result = mid_grad.astype(F32) + norm_back(upstream, in_hat, in_inverse, norm1_ref[...])
    out_ref[...] = from_quadrants(result).astype(BF16)

    def sent_all(e, carry):
        @pl.when(e != me)
        def _():
            ship_back(e).wait_send()

        return carry

    lax.fori_loop(0, E, sent_all, 0)
    for q in range(3):
        ship_quadrant(0, window_out, window_in, q, back[q]).wait_send()
        ship_quadrant(1, context_out, context_in, q, back[q]).wait_send()
        ship_quadrant(2, final_out, final_in, q + 1, ahead[q + 1]).wait_send()


def block(mid, grad, block_in, qkv, routes, w_in, w_out, w_qkv, w_proj, norm1, norm2):
    vmem = pl.BlockSpec(memory_space=pltpu.VMEM)
    anywhere = pl.BlockSpec(memory_space=pl.ANY)
    dma = pltpu.SemaphoreType.DMA
    return pl.pallas_call(
        block_kernel,
        out_shape=jax.ShapeDtypeStruct((256, 1024), BF16),
        in_specs=[vmem] * 5 + [anywhere] * 4 + [vmem] * 2,
        out_specs=vmem,
        scratch_shapes=[
            pltpu.VMEM((PIECES, 1024, HID), BF16),
            pltpu.VMEM((PIECES, HID, 1024), BF16),
            pltpu.VMEM((256, 1024), BF16),
            pltpu.VMEM((256, 1024), BF16),
            pltpu.VMEM((256, 128), F32),
            pltpu.VMEM((E, 2, C, 1024), BF16),
            pltpu.VMEM((E, 2, C, 1024), BF16),
            pltpu.VMEM((E * C, 1024), F32),
            pltpu.VMEM((E, C, 1024), BF16),
            pltpu.VMEM((256, E * C), BF16),
            pltpu.VMEM((2, E * C, HID), F32),
            pltpu.VMEM((HEADS // 4, 256, 1024), BF16),
            pltpu.VMEM((HEADS // 4, 128, 256), BF16),
            pltpu.VMEM((4, 3, 64, 1024), BF16),
            pltpu.VMEM((4, 3, 64, 1024), BF16),
            pltpu.VMEM((4, 64, 1024), BF16),
            pltpu.VMEM((4, 64, 1024), BF16),
            pltpu.VMEM((256, 3072), BF16),
            pltpu.VMEM((4, 64, 1024), BF16),
            pltpu.VMEM((4, 64, 1024), BF16),
            dma((8,)),
            dma((3, 4)),
            dma((3, 4)),
            dma((3,)),
            dma((3,)),
            dma((2, 8)),
            dma((2, 8)),
            dma((E,)),
            dma((E,)),
            dma((E,)),
            dma((E,)),
        ],
        compiler_params=pltpu.CompilerParams(
            collective_id=0, has_side_effects=True, vmem_limit_bytes=62 * 1024 * 1024
        ),
        name="block",
    )(mid, grad, block_in, qkv, routes, w_in, w_out, w_qkv, w_proj, norm1, norm2)


def shards(
    grad_out, block_in, mid, qkv, gates, expert_ids, w_in, w_out, w_qkv, w_proj, norm1, norm2
):
    window = grad_out.shape[2]
    width = grad_out.shape[4]
    count = window * window
    half = window // 2

    routes = jnp.concatenate((gates, expert_ids.astype(F32)), -1)
    routes = routes.reshape(2, half, 2, half, 4).transpose(0, 2, 1, 3, 4).reshape(count, 4)
    routes = jnp.pad(routes, ((0, 0), (0, 124)))
    result = block(
        mid.reshape(count, width),
        grad_out.reshape(count, width),
        block_in.reshape(count, width),
        qkv.reshape(window, window, 3, width).transpose(0, 2, 1, 3),
        routes,
        w_in[0],
        w_out[0],
        w_qkv,
        w_proj,
        norm1.reshape(1, width),
        norm2.reshape(1, width),
    )
    return result.reshape(grad_out.shape)


def solution(mesh):
    return jax.shard_map(
        shards,
        mesh=mesh,
        in_specs=(
            P("row", "col", None, None, None),
            P("row", "col", None, None, None),
            P("row", "col", None, None, None),
            P("row", "col", None, None, None, None),
            P("row", "col", None, None, None),
            P("row", "col", None, None, None),
            P(("row", "col"), None, None),
            P(("row", "col"), None, None),
            P(),
            P(),
            P(),
            P(),
        ),
        out_specs=P("row", "col", None, None, None),
        check_vma=False,
    )
```
